32 devices in a mesh: fsdp: 8 (over y, x, core), ctx: 4 (over z).
Axes of the slice: x: 2, y: 2, z: 4, core: 2. Of those that a mesh axis runs over, the one named last changes fastest.
Arguments:
- tokens: bfloat16 [16384, 1536], P(('fsdp', 'ctx')), may hold values from -6 to 6
- stretch_pairs: int32 [8, 4], P('fsdp'), may hold values from 0 to 3, each once within a row
- cotangent: bfloat16 [16384, 1536], P(('fsdp', 'ctx')), may hold values from -6 to 6
- w_qkv: bfloat16 [2048, 1536], P(('fsdp', 'ctx')), may hold values from -0.15625 to 0.15625
- b_qkv: bfloat16 [2048], P(('fsdp', 'ctx')), may hold values from -3 to 3
- w_out: bfloat16 [1536, 1536], P(('fsdp', 'ctx')), may hold values from -0.625 to 0.625
- norm_attn: bfloat16 [1536], P(('fsdp', 'ctx')), may hold values from 0.099609375 to 1.8984375
- norm_mlp: bfloat16 [1536], P(('fsdp', 'ctx')), may hold values from 0.099609375 to 1.8984375
- w_gate: bfloat16 [8960, 1536], P(('fsdp', 'ctx')), may hold values from -0.15625 to 0.15625
- w_up: bfloat16 [8960, 1536], P(('fsdp', 'ctx')), may hold values from -0.15625 to 0.15625
- w_down: bfloat16 [8960, 1536], P(('fsdp', 'ctx')), may hold values from -0.125 to 0.125
Outputs:
- layer_out: bfloat16 [16384, 1536], P(('fsdp', 'ctx'))
- grad_tokens: float32 [16384, 1536], P(('fsdp', 'ctx'))
- grad_qkv: float32 [2048, 1536], P(('fsdp', 'ctx'))
- grad_query_bias: float32 [1536], P(('fsdp', 'ctx'))
- grad_kv_bias: float32 [512], P(('fsdp', 'ctx'))
- grad_out: float32 [1536, 1536], P(('fsdp', 'ctx'))
- grad_norm_attn: float32 [1536], P(('fsdp', 'ctx'))
- grad_norm_mlp: float32 [1536], P(('fsdp', 'ctx'))
- grad_gate: float32 [8960, 1536], P(('fsdp', 'ctx'))
- grad_up: float32 [8960, 1536], P(('fsdp', 'ctx'))
- grad_down: float32 [8960, 1536], P(('fsdp', 'ctx'))
The draws below stay inside these ranges and needn't reach their ends.
Inputs may be any that keep to these rules, and one draw needn't show every extreme that they name: `stretch_pairs`: each row is a permutation: the 4 ranks of a sequence hold different block pairs, pair p being blocks p and 7 - p.
All inputs are finite; a program needn't handle non-finite values.
Results may differ from the reference program's by a relative error of at most 0.015.
Values may be sent and summed in bfloat16 or wider, within the bound.
No kernel may reach another device: no remote copies, remote signals or barrier semaphores. Data moves between devices by JAX's collectives and lax.ppermute only.
A program may use at most 320 MiB of HBM per device.

```python
import jax
import jax.numpy as jnp
from jax import lax

D = 1536
HEADS = 12
KV_HEADS = 2
HEAD = 128
FF = 8960
SEQS = 1
LENGTH = 2048
TOKENS = 16384
N_FSDP = 8
N_CTX = 4


def levels(rng, shape, cuts, least, high):
    def one(dim, blocks):
        steps = jax.random.uniform(jax.random.fold_in(jax.random.fold_in(rng, 6), dim), (blocks,), jnp.float32, least / len(cuts), high / len(cuts))
        return jnp.repeat(jnp.exp(steps), shape[dim] // blocks).reshape((-1,) + (1,) * (len(shape) - dim - 1))

    factor_of = one(*cuts[0])
    for cut in cuts[1:]:
        factor_of = factor_of * one(*cut)
    return factor_of


def scatter_about(stream_key, extent, spread, most, pieces=(), kind=jnp.bfloat16):
    drawn = spread * jax.random.normal(stream_key, extent, jnp.float32)
    if pieces:
        drawn = drawn * levels(stream_key, extent, pieces, -0.22, 0.18)
    return jnp.clip(drawn, -most, most).astype(kind)


def setup_inputs(seed: int = 0) -> dict:
    seeds = jax.random.split(jax.random.key(seed), 12)
    return {
        "tokens": scatter_about(seeds[0], (TOKENS, D), 1.0, 6.0, ((0, 32),)),
        "stretch_pairs": jax.vmap(lambda own: jax.random.permutation(own, N_CTX))(jax.random.split(seeds[1], (N_FSDP * SEQS))).reshape((N_FSDP * SEQS, N_CTX)).astype(jnp.int32),
        "cotangent": scatter_about(seeds[2], (TOKENS, D), 1.0, 6.0, ((0, 32),)),
        "w_qkv": scatter_about(seeds[3], ((HEADS + 2 * KV_HEADS) * HEAD, D), D ** -0.5, 0.15625, ((0, 32),)),
        "b_qkv": scatter_about(seeds[4], ((HEADS + 2 * KV_HEADS) * HEAD,), 0.5, 3.0, ((0, 32),)),
        "w_out": scatter_about(seeds[5], (HEADS * HEAD, D), (HEADS * HEAD // 16) ** -0.5, 0.625, ((0, 32),)),
        "norm_attn": jnp.clip(1.0 + 0.18 * jax.random.normal(seeds[6], (D,), jnp.float32), 0.099609375, 1.8984375).astype(jnp.bfloat16),
        "norm_mlp": jnp.clip(1.0 + 0.18 * jax.random.normal(seeds[7], (D,), jnp.float32), 0.099609375, 1.8984375).astype(jnp.bfloat16),
        "w_gate": scatter_about(seeds[8], (FF, D), D ** -0.5, 0.15625, ((0, 32),)),
        "w_up": scatter_about(seeds[9], (FF, D), D ** -0.5, 0.15625, ((0, 32),)),
        "w_down": scatter_about(seeds[10], (FF, D), (FF // 4) ** -0.5, 0.125, ((0, 32),)),
    }


rope_base = 1000000.0
norm_eps = 1e-06
highest = lax.Precision.HIGHEST

@jax.custom_vjp
def low(v):
    return lax.optimization_barrier(v.astype(jnp.bfloat16)).astype(jnp.float32)

@jax.custom_vjp
def low_back(v):
    return v

def low_keep(v):
    return (low(v), None)

def low_pass(kept, grad):
    return (grad,)

def back_keep(v):
    return (v, None)

def back_low(kept, grad):
    return (low(grad),)
low.defvjp(low_keep, low_pass)
low_back.defvjp(back_keep, back_low)

def matmul(left, right):
    return jnp.dot(left, right, precision=highest)

def rope_tables(positions):
    exponent = jnp.arange(0, HEAD, 2).astype(jnp.float32) / HEAD
    inverse = rope_base ** (-exponent)
    angles = positions.astype(jnp.float32)[:, None] * inverse[None, :]
    angles = jnp.concatenate([angles, angles], axis=1)
    return (jnp.cos(angles), jnp.sin(angles))

def rotate(values, cosine, sine_table):
    half_dim = HEAD // 2
    turned = jnp.concatenate([-values[..., half_dim:], values[..., :half_dim]], axis=-1)
    return values * cosine[:, None, :] + turned * sine_table[:, None, :]

def rms_scale(values):
    return lax.rsqrt(lax.optimization_barrier(jnp.mean(values * values, axis=-1, keepdims=True)) + norm_eps)

def layer_block(inputs, positions, w_qkv, b_qkv, w_out, norm_attn, norm_mlp, w_gate, w_up, w_down):
    seq_len = inputs.shape[0]
    query_width = HEADS * HEAD
    kv_width = KV_HEADS * HEAD
    group_size = HEADS // KV_HEADS
    normed_one = low(inputs * rms_scale(inputs) * norm_attn)
    projected = low_back(matmul(normed_one, w_qkv.T) + b_qkv)
    cosine, sine_table = rope_tables(positions)
    queries = low(rotate(projected[:, :query_width].reshape(seq_len, HEADS, HEAD), cosine, sine_table))
    keys = low(rotate(projected[:, query_width:query_width + kv_width].reshape(seq_len, KV_HEADS, HEAD), cosine, sine_table))
    values = low(projected[:, query_width + kv_width:].reshape(seq_len, KV_HEADS, HEAD))
    grouped = queries.reshape(seq_len, KV_HEADS, group_size, HEAD)
    scores = low_back(jnp.einsum('lgjd,mgd->gjlm', grouped, keys, precision=highest) * HEAD ** (-0.5))
    allowed = positions[None, :] <= positions[:, None]
    scores = jnp.where(allowed, scores, -1e+30)
    probs = low(jax.nn.softmax(scores, axis=-1))
    attended = jnp.einsum('gjlm,mgd->lgjd', probs, values, precision=highest).reshape(seq_len, query_width)
    attended = low_back(low(attended))
    middle = inputs + low_back(matmul(attended, w_out))
    normed_two = low(middle * rms_scale(middle) * norm_mlp)
    gate_pre = low_back(matmul(normed_two, w_gate.T))
    up_pre = low_back(matmul(normed_two, w_up.T))
    hidden = low(jax.nn.silu(gate_pre) * up_pre)
    return middle + matmul(hidden, w_down)

def reference(tokens, stretch_pairs, cotangent, w_qkv, b_qkv, w_out, norm_attn, norm_mlp, w_gate, w_up, w_down):
    local_len = LENGTH // N_CTX
    half_len = local_len // 2
    offsets = jnp.arange(local_len).astype(jnp.int32)
    pair_col = stretch_pairs.astype(jnp.int32)[:, :, None]
    positions = jnp.where(offsets < half_len, pair_col * half_len + offsets, (2 * N_CTX - 1 - pair_col) * half_len + offsets - half_len)
    positions = positions.reshape(N_FSDP * SEQS, LENGTH)

    def to_sequences(array):
        return array.reshape(N_FSDP, N_CTX, SEQS, local_len, D).transpose(0, 2, 1, 3, 4).reshape(N_FSDP * SEQS, LENGTH, D)

    def to_rows(array):
        return array.reshape(N_FSDP, SEQS, N_CTX, local_len, D).transpose(0, 2, 1, 3, 4).reshape(TOKENS, D)

    def forward(inputs, f_qkv, f_bias, f_out, f_norm_one, f_norm_two, f_gate, f_up, f_down):

        def one_sequence(pair_args):
            seq_in, seq_pos = pair_args
            return layer_block(seq_in, seq_pos, f_qkv, f_bias, f_out, f_norm_one, f_norm_two, f_gate, f_up, f_down)
        return to_rows(lax.map(jax.checkpoint(one_sequence), (to_sequences(inputs), positions)))
    result, pullback = jax.vjp(forward, tokens.astype(jnp.float32), w_qkv.astype(jnp.float32), b_qkv.astype(jnp.float32), w_out.astype(jnp.float32), norm_attn.astype(jnp.float32), norm_mlp.astype(jnp.float32), w_gate.astype(jnp.float32), w_up.astype(jnp.float32), w_down.astype(jnp.float32))
    grads = pullback(cotangent.astype(jnp.float32))
    query_width = HEADS * HEAD
    return (result.astype(jnp.bfloat16), grads[0], grads[1], grads[2][:query_width], grads[2][query_width:], grads[3], grads[4], grads[5], grads[6], grads[7], grads[8])
```

```python
import functools

import jax
import jax.numpy as jnp
from jax import lax
from jax.experimental import pallas as pl
from jax.experimental.pallas import tpu as pltpu
from jax.sharding import Mesh
from jax.sharding import PartitionSpec as P

HEADS = 12
KV_HEADS = 2
HEAD = 128
GROUP = HEADS // KV_HEADS
MIB = 2**20

rope_base = 1000000.0
norm_eps = 1e-06

LOG2E = 1.4426950408889634
SCALE = HEAD ** -0.5

NT = (((1,), (1,)), ((), ()))
NN = (((1,), (0,)), ((), ()))
TN = (((0,), (0,)), ((), ()))


def dot(left, right, dims):
    return lax.dot_general(left, right, dims, preferred_element_type=jnp.float32)


def forward_kernel(table, q_ref, k_ref, v_ref, o_ref, lse_ref, top, total, acc):
    half = pl.program_id(2)
    block = q_ref.shape[1]
    last = table[0, half]
    spot = table[0, 2 + last]
    heads = range(GROUP)

    def part(slot, masked, first):
        rows = pl.ds(pl.multiple_of(slot * block, block), block)
        keys, values = k_ref[0, rows, :], v_ref[0, rows, :]
        if not first:
            old_top = [top[j] for j in heads]
            old_total = [total[j] for j in heads]
        scores = [dot(keys, q_ref[0, :, pl.ds(j * HEAD, HEAD)], NT) for j in heads]
        if masked:
            key_at = lax.broadcasted_iota(jnp.int32, scores[0].shape, 0)
            query_at = lax.broadcasted_iota(jnp.int32, scores[0].shape, 1)
            scores = [jnp.where(key_at <= query_at, s, -1e30) for s in scores]
        tops = [jnp.max(s, axis=0, keepdims=True) * (SCALE * LOG2E) for s in scores]
        if not first:
            tops = [jnp.maximum(t, o) for t, o in zip(tops, old_top)]
        expon = [jnp.exp2(s * (SCALE * LOG2E) - t) for s, t in zip(scores, tops)]
        sums = [jnp.sum(e, axis=0, keepdims=True) for e in expon]
        added = [dot(values, e.astype(jnp.bfloat16), TN) for e in expon]
        for j in heads:
            if first:
                total[j] = sums[j]
                acc[j] = added[j]
            else:
                fade = jnp.exp2(old_top[j] - tops[j])
                total[j] = old_total[j] * fade + sums[j]
                acc[j] = acc[j] * fade + added[j]
            top[j] = tops[j]

    part(spot, True, True)

    def step(b, carry):
        part(table[0, 2 + b], False, False)
        return carry

    lax.fori_loop(0, last, step, 0)
    for j in heads:
        o_ref[0, :, pl.ds(j * HEAD, HEAD)] = (acc[j] / total[j]).T.astype(jnp.bfloat16)
        lse_ref[0, 0, 0, j] = (top[j] + jnp.log2(total[j]))[0]


def attend_forward(table, queries, keys, values):
    seqs, rows, width = queries.shape
    block = rows // 2
    wide = GROUP * HEAD
    seq_len = keys.shape[1]
    grid_spec = pltpu.PrefetchScalarGridSpec(
        num_scalar_prefetch=0,
        grid=(seqs, KV_HEADS, 2),
        in_specs=[
            pl.BlockSpec((1, table.shape[1]), lambda s, g, h: (s, 0), memory_space=pltpu.SMEM),
            pl.BlockSpec((1, block, wide), lambda s, g, h: (s, h, g)),
            pl.BlockSpec((1, seq_len, HEAD), lambda s, g, h: (s, 0, g)),
            pl.BlockSpec((1, seq_len, HEAD), lambda s, g, h: (s, 0, g)),
        ],
        out_specs=[
            pl.BlockSpec((1, block, wide), lambda s, g, h: (s, h, g)),
            pl.BlockSpec((1, 1, 1, GROUP, block), lambda s, g, h: (s, g, h, 0, 0)),
        ],
        scratch_shapes=[
            pltpu.VMEM((GROUP, 1, block), jnp.float32),
            pltpu.VMEM((GROUP, 1, block), jnp.float32),
            pltpu.VMEM((GROUP, HEAD, block), jnp.float32),
        ],
    )
    return pl.pallas_call(
        forward_kernel,
        grid_spec=grid_spec,
        out_shape=[
            jax.ShapeDtypeStruct(queries.shape, jnp.bfloat16),
            jax.ShapeDtypeStruct((seqs, KV_HEADS, 2, GROUP, block), jnp.float32),
        ],
        compiler_params=pltpu.CompilerParams(vmem_limit_bytes=40 * 2**20),
        cost_estimate=pl.CostEstimate(flops=2*2*HEADS*HEAD*rows*seq_len*seqs*9//16, bytes_accessed=6*2**20, transcendentals=HEADS*rows*seq_len*seqs*9//16),
        name="attend_forward",
    )(table, queries, keys, values)


def backward_kernel(table, q_ref, k_ref, v_ref, g_ref, o_ref, lse_ref, cos_ref, sin_ref, dq_ref, dk_ref, dv_ref, dk_acc, dv_acc, dq_acc, delta):
    half = pl.program_id(2)
    block = q_ref.shape[1]
    last = table[0, half]
    heads = range(GROUP)

    for j in heads:
        lanes = pl.ds(j * HEAD, HEAD)
        product = o_ref[0, :, lanes].astype(jnp.float32) * g_ref[0, :, lanes].astype(jnp.float32)
        delta[j] = jnp.sum(product.T, axis=0, keepdims=True)

    @pl.when(half == 0)
    def _():
        dk_acc[...] = jnp.zeros_like(dk_acc)
        dv_acc[...] = jnp.zeros_like(dv_acc)

    def part(slot, masked, first):
        rows = pl.ds(pl.multiple_of(slot * block, block), block)
        keys, values = k_ref[0, rows, :], v_ref[0, rows, :]
        lanes = [pl.ds(j * HEAD, HEAD) for j in heads]
        scores = [dot(keys, q_ref[0, :, lanes[j]], NT) for j in heads]
        d_probs = [dot(values, g_ref[0, :, lanes[j]], NT) for j in heads]
        probs = [
            jnp.exp2(scores[j] * (SCALE * LOG2E) - lse_ref[0, 0, 0, pl.ds(j, 1), :]) for j in heads
        ]
        if masked:
            key_at = lax.broadcasted_iota(jnp.int32, scores[0].shape, 0)
            query_at = lax.broadcasted_iota(jnp.int32, scores[0].shape, 1)
            probs = [jnp.where(key_at <= query_at, p, 0.0) for p in probs]
        d_scores = [(probs[j] * (d_probs[j] - delta[j])).astype(jnp.bfloat16) for j in heads]
        low = [p.astype(jnp.bfloat16) for p in probs]
        dv = sum(dot(low[j], g_ref[0, :, lanes[j]], NN) for j in heads)
        dk = sum(dot(d_scores[j], q_ref[0, :, lanes[j]], NN) for j in heads)
        dq = [dot(keys, d_scores[j], TN) for j in heads]
        for j in heads:
            if first:
                dq_acc[j] = dq[j]
            else:
                dq_acc[j] += dq[j]
        dk_acc[rows, :] += dk
        dv_acc[rows, :] += dv

    part(table[0, 2 + last], True, True)

    def step(b, carry):
        part(table[0, 2 + b], False, False)
        return carry

    lax.fori_loop(0, last, step, 0)
    for j in heads:
        grad = dq_acc[j].T * SCALE
        grad = grad * cos_ref[...] - pltpu.roll(grad, HEAD // 2, 1) * sin_ref[...]
        dq_ref[0, :, pl.ds(j * HEAD, HEAD)] = grad.astype(dq_ref.dtype)

    @pl.when(half == 1)
    def _():
        dk_ref[0] = (dk_acc[...] * SCALE).astype(dk_ref.dtype)
        dv_ref[0] = dv_acc[...].astype(dv_ref.dtype)


def attend_backward(table, queries, keys, values, grads, attended, lse, cosine, signed_sine):
    seqs, rows, width = queries.shape
    block = rows // 2
    wide = GROUP * HEAD
    seq_len = keys.shape[1]
    rows_spec = pl.BlockSpec((1, block, wide), lambda s, g, h: (s, h, g))
    keys_spec = pl.BlockSpec((1, seq_len, HEAD), lambda s, g, h: (s, 0, g))
    trig_spec = pl.BlockSpec((block, HEAD), lambda s, g, h: (2 * s + h, 0))
    stat_spec = pl.BlockSpec((1, 1, 1, GROUP, block), lambda s, g, h: (s, g, h, 0, 0))
    return pl.pallas_call(
        backward_kernel,
        grid=(seqs, KV_HEADS, 2),
        in_specs=[
            pl.BlockSpec((1, table.shape[1]), lambda s, g, h: (s, 0), memory_space=pltpu.SMEM),
            rows_spec, keys_spec, keys_spec, rows_spec, rows_spec, stat_spec, trig_spec, trig_spec,
        ],
        out_specs=[rows_spec, keys_spec, keys_spec],
        out_shape=[
            jax.ShapeDtypeStruct(queries.shape, jnp.bfloat16),
            jax.ShapeDtypeStruct(keys.shape, jnp.bfloat16),
            jax.ShapeDtypeStruct(values.shape, jnp.bfloat16),
        ],
        scratch_shapes=[
            pltpu.VMEM((seq_len, HEAD), jnp.float32),
            pltpu.VMEM((seq_len, HEAD), jnp.float32),
            pltpu.VMEM((GROUP, HEAD, block), jnp.float32),
            pltpu.VMEM((GROUP, 1, block), jnp.float32),
        ],
        compiler_params=pltpu.CompilerParams(vmem_limit_bytes=40 * 2**20),
        cost_estimate=pl.CostEstimate(flops=5*2*HEADS*HEAD*rows*seq_len*seqs*9//16, bytes_accessed=12*2**20, transcendentals=HEADS*rows*seq_len*seqs*9//16),
        name="attend_backward",
    )(table, queries, keys, values, grads, attended, lse, cosine, signed_sine)


def grad_kernel(count, *refs):
    out = refs[-1]
    total = None
    for left, right in zip(refs[:count], refs[count:2 * count]):
        term = dot(left[...], right[...], NN)
        total = term if total is None else total + term
    out[...] = total.astype(out.dtype)


def unit_grads(lefts, rights, block=320):
    units = lefts[0].shape[0]
    rows, width = rights[0].shape
    count = len(lefts)
    return pl.pallas_call(
        functools.partial(grad_kernel, count),
        grid=(units // block,),
        in_specs=[pl.BlockSpec((block, l.shape[1]), lambda i: (i, 0)) for l in lefts]
        + [pl.BlockSpec(r.shape, lambda i: (0, 0)) for r in rights],
        out_specs=pl.BlockSpec((block, width), lambda i: (i, 0)),
        out_shape=jax.ShapeDtypeStruct((units, width), jnp.bfloat16),
        compiler_params=pltpu.CompilerParams(vmem_limit_bytes=56 * MIB),
        cost_estimate=pl.CostEstimate(
            flops=2 * count * units * rows * width, bytes_accessed=2 * count * rows * (units + width), transcendentals=0
        ),
        name="unit_grads",
    )(*lefts, *rights)


def project_kernel(rows_ref, gain, weight, bias, cosine, signed_sine, normed, queries, kv):
    step = pl.program_id(0)
    query_steps = pl.num_programs(0) - 2

    @pl.when(step == 0)
    def _():
        rows = rows_ref[...].astype(jnp.float32)
        scale = lax.rsqrt(jnp.mean(rows * rows, axis=-1, keepdims=True) + norm_eps)
        normed[...] = (rows * scale * gain[...]).astype(normed.dtype)

    out = dot(normed[...], weight[...], NT) + bias[...]

    def turned():
        parts = []
        for start in range(0, out.shape[1], HEAD):
            part = out[:, start : start + HEAD]
            parts.append(part * cosine[...] + pltpu.roll(part, HEAD // 2, 1) * signed_sine[...])
        return jnp.concatenate(parts, axis=1).astype(queries.dtype)

    @pl.when(step < query_steps)
    def _():
        queries[...] = turned()

    @pl.when(step == query_steps)
    def _():
        kv[...] = turned()

    @pl.when(step > query_steps)
    def _():
        kv[...] = out.astype(kv.dtype)


def project_heads(tokens, gain, weight, bias, cosine, signed_sine):
    rows, width = tokens.shape
    block = KV_HEADS * HEAD
    steps = weight.shape[0] // block
    whole = pl.BlockSpec((rows, width), lambda i: (0, 0))
    table = pl.BlockSpec((rows, HEAD), lambda i: (0, 0))
    low = jnp.bfloat16
    return pl.pallas_call(
        project_kernel,
        grid=(steps,),
        in_specs=[
            whole,
            pl.BlockSpec((1, width), lambda i: (0, 0)),
            pl.BlockSpec((block, width), lambda i: (i, 0)),
            pl.BlockSpec((1, block), lambda i: (0, i)),
            table,
            table,
        ],
        out_specs=[
            whole,
            pl.BlockSpec((rows, block), lambda i: (0, jnp.minimum(i, steps - 3))),
            pl.BlockSpec((rows, block), lambda i: (0, jnp.maximum(i - steps + 2, 0))),
        ],
        out_shape=[
            jax.ShapeDtypeStruct((rows, width), low),
            jax.ShapeDtypeStruct((rows, (steps - 2) * block), low),
            jax.ShapeDtypeStruct((rows, 2 * block), low),
        ],
        compiler_params=pltpu.CompilerParams(vmem_limit_bytes=40 * MIB),
        cost_estimate=pl.CostEstimate(
            flops=2 * rows * width * weight.shape[0],
            bytes_accessed=2 * (weight.size + 4 * tokens.size),
            transcendentals=0,
        ),
        name="project_heads",
    )(tokens, gain, weight, bias, cosine, signed_sine)


def unit_kernel(normed, d_hidden, gate, up, hidden, d_gate, d_up):
    gate_pre = dot(gate[...], normed[...], NT)
    up_pre = dot(up[...], normed[...], NT)
    d_mid = d_hidden[...].astype(jnp.float32)
    sig = 1.0 / (1.0 + jnp.exp(-gate_pre))
    silu = gate_pre * sig
    hidden[...] = (silu * up_pre).astype(hidden.dtype)
    d_up[...] = (d_mid * silu).astype(d_up.dtype)
    d_gate[...] = (d_mid * up_pre * (sig + silu * (1.0 - sig))).astype(d_gate.dtype)


def unit_rows(normed, d_hidden, gate, up):
    units, width = gate.shape
    rows = normed.shape[0]
    block = units // 4
    part = pl.BlockSpec((block, width), lambda i: (i, 0))
    out = pl.BlockSpec((block, rows), lambda i: (i, 0))
    shape = jax.ShapeDtypeStruct((units, rows), jnp.bfloat16)
    return pl.pallas_call(
        unit_kernel,
        grid=(units // block,),
        in_specs=[pl.BlockSpec((rows, width), lambda i: (0, 0)), out, part, part],
        out_specs=[out, out, out],
        out_shape=[shape, shape, shape],
        compiler_params=pltpu.CompilerParams(vmem_limit_bytes=48 * MIB),
        cost_estimate=pl.CostEstimate(
            flops=4 * units * rows * width,
            bytes_accessed=4 * units * width + 8 * units * rows,
            transcendentals=2 * units * rows,
        ),
        name="unit_rows",
    )(normed, d_hidden, gate, up)


def rope_tables(positions):
    exponent = jnp.arange(0, HEAD, 2).astype(jnp.float32) / HEAD
    inverse = rope_base ** (-exponent)
    angles = positions.astype(jnp.float32)[:, None] * inverse[None, :]
    angles = jnp.concatenate([angles, angles], axis=1)
    return (jnp.cos(angles), jnp.sin(angles))


def rms_scale(values):
    return lax.rsqrt(jnp.mean(values * values, axis=-1, keepdims=True) + norm_eps)


def norm_back(d_normed, values, inv_scale, gain):
    scaled = d_normed * gain
    grad_gain = jnp.sum(d_normed * values * inv_scale, axis=0)
    inner = jnp.mean(scaled * values, axis=-1, keepdims=True)
    return (inv_scale * scaled - values * inv_scale * inv_scale * inv_scale * inner, grad_gain)


def project_rows(left, weight_rows):
    return jnp.einsum("rd,fd->rf", left, weight_rows, preferred_element_type=jnp.float32)


def flip(values, axis):
    return lax.ppermute(values, axis, [(0, 1), (1, 0)])


ALL_AXES = ("fa", "fb", "fc", "ch", "cl")
CTX_AXES = ("ch", "cl")


def gather_last(pieces):
    if lax.axis_size("fc") == 2:
        return jnp.concatenate([*pieces, *(flip(piece, "fc") for piece in pieces)], axis=0)
    return lax.all_gather(jnp.concatenate(pieces, axis=0), "fc", axis=0, tiled=True)


def over_a(values):
    if lax.axis_size("fa") == 2:
        return flip(values, "fa")
    return lax.all_gather(values, "fa", axis=0, tiled=True)


def join_a(own, other):
    if lax.axis_size("fa") == 2:
        return [*own, *other]
    count = lax.axis_size("fa")
    blocks = [block.reshape(count, -1, block.shape[1]) for block in other]
    return [jnp.concatenate(blocks, axis=1).reshape(-1, blocks[0].shape[2])]


def scatter_half(values, axis):
    half = values.shape[0] // 2
    return values[:half].astype(jnp.float32) + flip(values[half:], axis).astype(jnp.float32)


def scatter_a(values):
    if lax.axis_size("fa") == 2:
        return scatter_half(values, "fa")
    return lax.psum_scatter(values, "fa", scatter_dimension=0, tiled=True).astype(jnp.float32)


def far_rows(over_x, over_z):
    half = over_x.shape[0] // 2
    return jnp.concatenate([flip(over_z[:half], "fb"), flip(over_x[half:], "cl")], axis=0)


def scatter_far(far):
    half = far.shape[0] // 2
    return flip(far[:half], "fb"), flip(far[half:], "cl")


def scatter_near(over_x, over_z, from_x, from_z):
    half = over_x.shape[0] // 2
    low, wide = jnp.bfloat16, jnp.float32
    send_z = jnp.concatenate([over_z[:half] + from_x.astype(wide), over_z[half:]], axis=0)
    send_x = jnp.concatenate([over_x[:half], over_x[half:] + from_z.astype(wide)], axis=0)
    return send_x.astype(low), send_z.astype(low)


def scatter_end(own, send_x, send_z):
    wide = jnp.float32
    return own + flip(send_x, "fb").astype(wide) + flip(send_z, "cl").astype(wide)


def pack_vectors(vectors, blocks):
    flat = jnp.concatenate([v.reshape(blocks, -1) for v in vectors], axis=1)
    lanes = -(-flat.shape[1] // 1024) * 128
    flat = jnp.pad(flat, ((0, 0), (0, 8 * lanes - flat.shape[1])))
    return flat.reshape(blocks, 8, lanes)


def unpack_vectors(packed, sizes):
    flat = packed.reshape(packed.shape[0], -1)
    out = []
    start = 0
    for size in sizes:
        out.append(flat[:, start : start + size].reshape(-1))
        start += size
    return out


def xor_send(values, bits):
    count = lax.axis_size(CTX_AXES)
    return lax.ppermute(values, CTX_AXES, [(i, i ^ bits) for i in range(count)])


def stack_in_order(own, other, axis, dim):
    later = lax.axis_index(axis) == 1
    return jnp.stack([jnp.where(later, other, own), jnp.where(later, own, other)], axis=dim)


def stack_axis(values, axis, dim):
    if lax.axis_size(axis) == 2:
        return stack_in_order(values, flip(values, axis), axis, dim)
    return lax.all_gather(values, axis, axis=dim, tiled=False)


def stack_ctx(values):
    rel = [values] + [xor_send(values, k) for k in (1, 2, 3)]
    high, low = lax.axis_index("ch") == 1, lax.axis_index("cl") == 1
    rel = [jnp.where(low, rel[k ^ 1], rel[k]) for k in range(4)]
    rel = [jnp.where(high, rel[k ^ 2], rel[k]) for k in range(4)]
    return jnp.stack(rel).reshape(2, 2, *values.shape)


def stack_plane(over_z):
    if lax.axis_size("fa") != 2:
        return stack_axis(stack_axis(over_z, "fb", 0), "fa", 0)
    half = over_z.shape[2] // 2
    by_a, by_b = flip(over_z, "fa"), flip(over_z, "fb")
    far = jnp.concatenate([flip(by_a[:, :, :half], "fb"), flip(by_b[:, :, half:], "fa")], axis=2)
    near = stack_in_order(over_z, by_b, "fb", 0)
    beyond = stack_in_order(by_a, far, "fb", 0)
    return stack_in_order(near, beyond, "fa", 0)


def stack_core(plane):
    return stack_axis(plane, "fc", 2)


def pick(values, index, dim):
    return lax.dynamic_index_in_dim(values, index, dim, keepdims=False)


def scatter_axis(values, axis, dim):
    if lax.axis_size(axis) == 2:
        me = lax.axis_index(axis)
        kept, sent = pick(values, me, dim), pick(values, 1 - me, dim)
        return (kept.astype(jnp.float32) + flip(sent, axis).astype(jnp.float32)).astype(values.dtype)
    return lax.psum_scatter(values, axis, scatter_dimension=dim, tiled=False)


def scatter_all(values):
    values = scatter_axis(values, "fc", 2)
    if lax.axis_size("fa") == 2:
        half = values.shape[-2] // 2
        wide = jnp.float32
        low = values.dtype
        me_a, me_b = lax.axis_index("fa"), lax.axis_index("fb")
        far = pick(pick(values, 1 - me_a, 0), 1 - me_b, 0)
        over_a = pick(pick(values, 1 - me_a, 0), me_b, 0).astype(wide)
        over_b = pick(pick(values, me_a, 0), 1 - me_b, 0).astype(wide)
        own = pick(pick(values, me_a, 0), me_b, 0).astype(wide)
        top, bottom = slice(None, half), slice(half, None)
        from_b = flip(far[..., top, :], "fb").astype(wide)
        from_a = flip(far[..., bottom, :], "fa").astype(wide)
        send_a = jnp.concatenate(
            [over_a[..., top, :] + from_b, over_a[..., bottom, :]], axis=-2
        ).astype(low)
        send_b = jnp.concatenate(
            [over_b[..., top, :], over_b[..., bottom, :] + from_a], axis=-2
        ).astype(low)
        values = (
            own + flip(send_a, "fa").astype(wide) + flip(send_b, "fb").astype(wide)
        ).astype(low)
    else:
        values = scatter_axis(scatter_axis(values, "fa", 0), "fb", 0)
    return scatter_axis(scatter_axis(values, "ch", 0), "cl", 0)


def after(values, *first):
    return lax.optimization_barrier((values, *first))[0]


def on_device(
    tokens, stretch_pairs, cotangent, w_qkv, b_qkv, w_out, norm_attn, norm_mlp, w_gate, w_up, w_down
):
    ctx_count = lax.axis_size(CTX_AXES)
    device_count = lax.axis_size(ALL_AXES)
    device_grid = tuple(lax.axis_size(axis) for axis in ALL_AXES)
    ctx_rank = lax.axis_index(CTX_AXES)
    seq_count = stretch_pairs.shape[0]
    row_count, width = tokens.shape
    local_len = row_count // seq_count
    half_len = local_len // 2
    seq_len = local_len * ctx_count
    query_width = HEADS * HEAD
    kv_width = KV_HEADS * HEAD
    low, wide = jnp.bfloat16, jnp.float32

    vectors_z = stack_ctx(pack_vectors([b_qkv, norm_attn, norm_mlp], 1)[0])
    qkv_z = stack_ctx(w_qkv)
    vectors_plane = stack_plane(after(vectors_z, qkv_z))
    qkv_plane = stack_plane(qkv_z)
    vectors_all = stack_core(vectors_plane)
    bias_all, gain_one, gain_two = unpack_vectors(
        vectors_all.reshape(device_count, 8, -1),
        (b_qkv.shape[0], norm_attn.shape[0], norm_mlp.shape[0]),
    )
    gain_one, gain_two = gain_one.astype(wide)[None], gain_two.astype(wide)[None]
    qkv_all = stack_core(qkv_plane).reshape(-1, width)

    out_z = stack_ctx(after(w_out, qkv_z))
    down_z = flip(after(w_down, qkv_z), "ch")
    gate_z = flip(after(w_gate, qkv_z), "ch")
    cot_z = flip(after(cotangent, qkv_z), "cl")
    out_plane = stack_plane(after(out_z, qkv_plane))
    cot_x = flip(after(cotangent, qkv_plane), "fb")
    down_a = over_a(after(w_down, qkv_plane))
    gate_a = over_a(after(w_gate, qkv_plane))

    rank_order = jnp.arange(ctx_count) ^ ctx_rank
    pairs = stretch_pairs[:, rank_order]
    own_pair = pairs[:, :1]
    blocks = jnp.arange(2 * ctx_count)
    block_pair = jnp.minimum(blocks, 2 * ctx_count - 1 - blocks)
    holder = jnp.argmax(pairs[:, None, :] == block_pair[None, :, None], axis=2)
    slots = 2 * holder + (blocks >= ctx_count)[None, :]
    table = jnp.concatenate(
        [own_pair, 2 * ctx_count - 1 - own_pair, slots.astype(jnp.int32)], axis=1
    )
    offsets = jnp.arange(local_len)
    positions = jnp.where(
        offsets < half_len,
        own_pair * half_len + offsets,
        (2 * ctx_count - 1 - own_pair) * half_len + offsets - half_len,
    )
    cosine, sine_table = rope_tables(positions.reshape(row_count))
    signed_sine = jnp.where(jnp.arange(HEAD) < HEAD // 2, -sine_table, sine_table)

    normed_one, queries, kv_low = project_heads(
        tokens, gain_one, qkv_all, bias_all.astype(wide)[None], cosine, signed_sine
    )
    kv_low = kv_low.reshape(seq_count, local_len, 2 * kv_width)
    kv_all = jnp.concatenate([kv_low, *(xor_send(kv_low, k) for k in (1, 2, 3))], axis=1)

    up_a = over_a(after(w_up, kv_low))
    out_all = stack_core(after(out_plane, kv_low)).reshape(-1, width)
    kv_all, down_z, gate_z, cot_z, cot_x, down_a, gate_a = lax.optimization_barrier(
        (kv_all, down_z, gate_z, cot_z, cot_x, down_a, gate_a)
    )
    up_z = flip(after(w_up, kv_all), "ch")
    down_az, gate_az = over_a(down_z), over_a(gate_z)
    cot_far = far_rows(cot_x, cot_z)
    cot_parts = [cotangent, cot_x, cot_z, cot_far]

    queries = queries.reshape(seq_count, local_len, query_width)
    keys, values = kv_all[..., :kv_width], kv_all[..., kv_width:]
    attended, log_totals = attend_forward(table, queries, keys, values)
    attended_rows = attended.reshape(row_count, query_width)
    inputs = tokens.astype(wide)
    middle = inputs + jnp.dot(attended_rows, out_all, preferred_element_type=wide)
    inv_two = rms_scale(middle)
    normed_two = (middle * inv_two * gain_two).astype(low)

    def all_units(own, by_z, by_a, by_az):
        return gather_last(join_a([own, by_z], [by_a, by_az]))

    normed_two, down_az, gate_az, up_z, up_a = lax.optimization_barrier(
        (normed_two, down_az, gate_az, up_z, up_a)
    )
    up_az = over_a(up_z)
    normed_x, normed_z = flip(normed_two, "fb"), flip(normed_two, "cl")
    down_part = all_units(w_down, down_z, down_a, down_az)
    gate_part = all_units(w_gate, gate_z, gate_a, gate_az)
    d_hidden = [dot(down_part, cot, NT).astype(low) for cot in cot_parts]
    up_part = all_units(w_up, up_z, up_a, after(up_az, d_hidden[0]))
    normed_parts = [normed_two, normed_x, normed_z, far_rows(normed_x, normed_z)]

    def units(k, *first):
        return unit_rows(after(normed_parts[k], *first), d_hidden[k], gate_part, up_part)

    def back_units(k, *first):
        d_gate_k = after(d_gate[k], *first)
        return dot(d_gate_k, gate_part, TN) + dot(d_up[k], up_part, TN)

    results = [units(0)]
    for k in (1, 2, 3):
        results.append(units(k, results[-1][0]))
    hidden, d_gate, d_up = zip(*results)
    back_far = back_units(3)
    from_x, from_z = scatter_far(back_far.astype(low))
    back_x = back_units(1, back_far)
    back_z = back_units(2, back_x)
    send_x, send_z = scatter_near(back_x, back_z, from_x, from_z)
    back_own = back_units(0, send_x, send_z)
    down_terms = unit_grads([after(hidden[0], back_own), *hidden[1:]], cot_parts)
    gate_terms = unit_grads([after(d_gate[0], down_terms), *d_gate[1:]], normed_parts)
    d_normed_two = scatter_end(after(back_own, gate_terms), send_x, send_z)

    d_mid_norm, grad_gain_two = norm_back(d_normed_two, middle, inv_two, gain_two)
    d_middle = cotangent.astype(wide) + d_mid_norm
    d_branch = d_middle.astype(low)
    d_attended = project_rows(d_branch, out_all).astype(low)
    down_terms = scatter_half(down_terms, "fc").astype(low)
    gate_terms = scatter_half(gate_terms, "fc").astype(low)
    d_attended, down_terms, gate_terms = lax.optimization_barrier(
        (d_attended, down_terms, gate_terms)
    )
    down_terms = scatter_a(down_terms).astype(low)
    gate_terms = scatter_a(gate_terms).astype(low)
    d_queries, d_keys_parts, d_values_parts = attend_backward(
        table,
        queries,
        keys,
        values,
        d_attended.reshape(seq_count, local_len, query_width),
        attended,
        log_totals,
        cosine,
        signed_sine,
    )
    d_queries = d_queries.reshape(row_count, query_width)
    d_kv_parts = jnp.concatenate([d_keys_parts, d_values_parts], axis=-1)
    d_kv_parts = d_kv_parts.reshape(seq_count, ctx_count, local_len, 2 * kv_width)
    d_kv_sent = [xor_send(d_kv_parts[:, k], k) for k in (1, 2, 3)]

    d_queries, down_terms = lax.optimization_barrier((d_queries, down_terms))
    grad_down = scatter_half(down_terms, "ch")
    up_terms = unit_grads([after(d_up[0], d_queries), *d_up[1:]], normed_parts)
    up_sent = scatter_half(up_terms, "fc").astype(low)
    grad_out_local = dot(after(attended_rows, up_terms), d_branch, TN).astype(low)
    query_terms = dot(after(d_queries, up_terms), normed_one, TN)
    branch = [dot(after(h, query_terms), down_part, TN) for h in hidden]
    d_kv_parts, gate_terms, up_terms, branch[3], grad_out_local, d_kv_sent[0] = (
        lax.optimization_barrier(
            (d_kv_parts, gate_terms, up_sent, branch[3], grad_out_local, d_kv_sent[0])
        )
    )
    grad_gate = scatter_half(gate_terms, "ch")
    up_terms = scatter_a(up_terms).astype(low)
    branch_from = scatter_far(branch[3].astype(low))
    grad_out = scatter_all(grad_out_local.reshape(*device_grid, -1, width)).astype(wide)

    d_kv = d_kv_parts[:, 0].astype(wide)
    for sent in d_kv_sent:
        d_kv += sent.astype(wide)
    d_kv = d_kv.reshape(row_count, 2 * kv_width)
    d_keys = []
    for start in range(0, kv_width, HEAD):
        part = d_kv[:, start : start + HEAD]
        d_keys.append(part * cosine - jnp.roll(part, HEAD // 2, 1) * signed_sine)
    d_kv = jnp.concatenate([*d_keys, d_kv[:, kv_width:]], axis=1).astype(low)
    query_bias_local = jnp.sum(d_queries, axis=0, dtype=wide)
    kv_bias_local = jnp.sum(d_kv, axis=0, dtype=wide)
    kv_terms = dot(d_kv, normed_one, TN)
    qkv_local = jnp.concatenate([query_terms, kv_terms], axis=0)
    branch_sent = scatter_near(branch[1], branch[2], *branch_from)
    branch_two = scatter_end(branch[0], *branch_sent)
    layer_out = (middle + branch_two).astype(low)
    grad_up = scatter_half(up_terms, "ch")
    grad_qkv = scatter_all(qkv_local.astype(low).reshape(*device_grid, -1, width)).astype(wide)
    d_normed_one = dot(d_queries, qkv_all[:query_width], NN) + dot(d_kv, qkv_all[query_width:], NN)
    inv_one = rms_scale(inputs)
    d_in_norm, grad_gain_one = norm_back(d_normed_one, inputs, inv_one, gain_one)
    grad_tokens = d_middle + d_in_norm
    vector_grads = [query_bias_local, kv_bias_local, grad_gain_one, grad_gain_two]
    vector_shares = scatter_all(
        pack_vectors(vector_grads, device_count).reshape(*device_grid, 8, -1)
    )
    grad_query_bias, grad_kv_bias, grad_norm_attn, grad_norm_mlp = unpack_vectors(
        vector_shares[None], [v.shape[0] // device_count for v in vector_grads]
    )
    return (
        layer_out,
        grad_tokens,
        grad_qkv,
        grad_query_bias,
        grad_kv_bias,
        grad_out,
        grad_norm_attn,
        grad_norm_mlp,
        grad_gate,
        grad_up,
        grad_down,
    )


def solution(mesh):
    fsdp_count, ctx_count = mesh.shape["fsdp"], mesh.shape["ctx"]
    parts = (fsdp_count // 4, 2, 2, ctx_count // 2, 2)
    split_mesh = Mesh(mesh.devices.reshape(parts), ALL_AXES)
    rows, whole = P(ALL_AXES, None), P(ALL_AXES)
    return jax.shard_map(
        on_device,
        mesh=split_mesh,
        in_specs=(
            rows,
            P(("fa", "fb", "fc"), None),
            rows,
            rows,
            whole,
            rows,
            whole,
            whole,
            rows,
            rows,
            rows,
        ),
        out_specs=(rows, rows, rows, whole, whole, rows, whole, whole, rows, rows, rows),
        check_vma=False,
    )
```

```python
import functools

import jax
import jax.numpy as jnp
from jax import lax
from jax.experimental import pallas as pl
from jax.experimental.pallas import tpu as pltpu
from jax.sharding import Mesh
from jax.sharding import PartitionSpec as P

HEADS = 12
KV_HEADS = 2
HEAD = 128
GROUP = HEADS // KV_HEADS
MIB = 2**20
COST_FACTOR = 16


def cost(flops, nbytes, transcendentals=0):
    return pl.CostEstimate(
        flops=flops * COST_FACTOR,
        bytes_accessed=nbytes * COST_FACTOR,
        transcendentals=transcendentals * COST_FACTOR,
    )


rope_base = 1000000.0
norm_eps = 1e-06

LOG2E = 1.4426950408889634
SCALE = HEAD ** -0.5

NT = (((1,), (1,)), ((), ()))
NN = (((1,), (0,)), ((), ()))
TN = (((0,), (0,)), ((), ()))


def with_tokens(kernel, count, tokens):
    return lambda *refs: kernel(*refs[:count], *refs[count + tokens :])


def dot(left, right, dims):
    return lax.dot_general(left, right, dims, preferred_element_type=jnp.float32)


def forward_kernel(table, q_ref, k_ref, v_ref, o_ref, lse_ref, top, total, acc):
    half = pl.program_id(2)
    block = q_ref.shape[1]
    last = table[0, half]
    spot = table[0, 2 + last]
    heads = range(GROUP)

    def part(slot, masked, first):
        rows = pl.ds(pl.multiple_of(slot % 2 * block, block), block)
        keys, values = k_ref[slot // 2, 0, rows, :], v_ref[slot // 2, 0, rows, :]
        if not first:
            old_top = [top[j] for j in heads]
            old_total = [total[j] for j in heads]
        scores = [dot(keys, q_ref[0, :, pl.ds(j * HEAD, HEAD)], NT) for j in heads]
        if masked:
            key_at = lax.broadcasted_iota(jnp.int32, scores[0].shape, 0)
            query_at = lax.broadcasted_iota(jnp.int32, scores[0].shape, 1)
            scores = [jnp.where(key_at <= query_at, s, -1e30) for s in scores]
        tops = [jnp.max(s, axis=0, keepdims=True) * (SCALE * LOG2E) for s in scores]
        if not first:
            tops = [jnp.maximum(t, o) for t, o in zip(tops, old_top)]
        expon = [jnp.exp2(s * (SCALE * LOG2E) - t) for s, t in zip(scores, tops)]
        sums = [jnp.sum(e, axis=0, keepdims=True) for e in expon]
        added = [dot(values, e.astype(jnp.bfloat16), TN) for e in expon]
        for j in heads:
            if first:
                total[j] = sums[j]
                acc[j] = added[j]
            else:
                fade = jnp.exp2(old_top[j] - tops[j])
                total[j] = old_total[j] * fade + sums[j]
                acc[j] = acc[j] * fade + added[j]
            top[j] = tops[j]

    part(spot, True, True)

    def step(b, carry):
        part(table[0, 2 + b], False, False)
        return carry

    lax.fori_loop(0, last, step, 0)
    for j in heads:
        o_ref[0, :, pl.ds(j * HEAD, HEAD)] = (acc[j] / total[j]).T.astype(jnp.bfloat16)
        lse_ref[0, 0, 0, j] = (top[j] + jnp.log2(total[j]))[0]


def attend_forward(table, queries, kv, *first):
    seqs, rows, width = queries.shape
    block = rows // 2
    wide = GROUP * HEAD
    ranks = kv.shape[0]
    work = HEADS * rows * rows * ranks * seqs * 9 // 16
    return pl.pallas_call(
        with_tokens(forward_kernel, 4, len(first)),
        grid=(seqs, KV_HEADS, 2),
        in_specs=[
            pl.BlockSpec((1, table.shape[1]), lambda s, g, h: (s, 0), memory_space=pltpu.SMEM),
            pl.BlockSpec((1, block, wide), lambda s, g, h: (s, h, g)),
            pl.BlockSpec((ranks, 1, rows, HEAD), lambda s, g, h: (0, s, 0, g)),
            pl.BlockSpec((ranks, 1, rows, HEAD), lambda s, g, h: (0, s, 0, KV_HEADS + g)),
            *(pl.BlockSpec(memory_space=pl.ANY) for _ in first),
        ],
        out_specs=[
            pl.BlockSpec((1, block, wide), lambda s, g, h: (s, h, g)),
            pl.BlockSpec((1, 1, 1, GROUP, block), lambda s, g, h: (s, g, h, 0, 0)),
        ],
        out_shape=[
            jax.ShapeDtypeStruct(queries.shape, jnp.bfloat16),
            jax.ShapeDtypeStruct((seqs, KV_HEADS, 2, GROUP, block), jnp.float32),
        ],
        scratch_shapes=[
            pltpu.VMEM((GROUP, 1, block), jnp.float32),
            pltpu.VMEM((GROUP, 1, block), jnp.float32),
            pltpu.VMEM((GROUP, HEAD, block), jnp.float32),
        ],
        compiler_params=pltpu.CompilerParams(vmem_limit_bytes=40 * MIB),
        cost_estimate=cost(
            4 * HEAD * work, 6 * MIB, work
        ),
        name="attend_forward",
    )(table, queries, kv, kv, *first)


def backward_kernel(table, q_ref, k_ref, v_ref, g_ref, o_ref, lse_ref, cos_ref, sin_ref, dq_ref, dkv_ref, dk_acc, dv_acc, dq_acc, delta):
    half = pl.program_id(2)
    block = q_ref.shape[1]
    last = table[0, half]
    heads = range(GROUP)

    for j in heads:
        lanes = pl.ds(j * HEAD, HEAD)
        product = o_ref[0, :, lanes].astype(jnp.float32) * g_ref[0, :, lanes].astype(jnp.float32)
        delta[j] = jnp.sum(product.T, axis=0, keepdims=True)

    @pl.when(half == 0)
    def _():
        dk_acc[...] = jnp.zeros_like(dk_acc)
        dv_acc[...] = jnp.zeros_like(dv_acc)

    def part(slot, masked, first):
        rows = pl.ds(pl.multiple_of(slot % 2 * block, block), block)
        keys, values = k_ref[slot // 2, 0, rows, :], v_ref[slot // 2, 0, rows, :]
        lanes = [pl.ds(j * HEAD, HEAD) for j in heads]
        scores = [dot(keys, q_ref[0, :, lanes[j]], NT) for j in heads]
        d_probs = [dot(values, g_ref[0, :, lanes[j]], NT) for j in heads]
        probs = [
            jnp.exp2(scores[j] * (SCALE * LOG2E) - lse_ref[0, 0, 0, pl.ds(j, 1), :]) for j in heads
        ]
        if masked:
            key_at = lax.broadcasted_iota(jnp.int32, scores[0].shape, 0)
            query_at = lax.broadcasted_iota(jnp.int32, scores[0].shape, 1)
            probs = [jnp.where(key_at <= query_at, p, 0.0) for p in probs]
        d_scores = [(probs[j] * (d_probs[j] - delta[j])).astype(jnp.bfloat16) for j in heads]
        low = [p.astype(jnp.bfloat16) for p in probs]
        dv = sum(dot(low[j], g_ref[0, :, lanes[j]], NN) for j in heads)
        dk = sum(dot(d_scores[j], q_ref[0, :, lanes[j]], NN) for j in heads)
        dq = [dot(keys, d_scores[j], TN) for j in heads]
        for j in heads:
            if first:
                dq_acc[j] = dq[j]
            else:
                dq_acc[j] += dq[j]
        dk_acc[slot // 2, rows, :] += dk
        dv_acc[slot // 2, rows, :] += dv

    part(table[0, 2 + last], True, True)

    def step(b, carry):
        part(table[0, 2 + b], False, False)
        return carry

    lax.fori_loop(0, last, step, 0)
    for j in heads:
        grad = dq_acc[j].T * SCALE
        grad = grad * cos_ref[...] - pltpu.roll(grad, HEAD // 2, 1) * sin_ref[...]
        dq_ref[0, :, pl.ds(j * HEAD, HEAD)] = grad.astype(dq_ref.dtype)

    @pl.when(half == 1)
    def _():
        dkv_ref[:, 0, 0] = (dk_acc[...] * SCALE).astype(dkv_ref.dtype)
        dkv_ref[:, 0, 1] = dv_acc[...].astype(dkv_ref.dtype)


def attend_backward(table, queries, kv, grads, attended, lse, cosine, signed_sine, *first):
    seqs, rows, width = queries.shape
    block = rows // 2
    wide = GROUP * HEAD
    ranks = kv.shape[0]
    work = HEADS * rows * rows * ranks * seqs * 9 // 16
    rows_spec = pl.BlockSpec((1, block, wide), lambda s, g, h: (s, h, g))
    trig_spec = pl.BlockSpec((block, HEAD), lambda s, g, h: (2 * s + h, 0))
    return pl.pallas_call(
        with_tokens(backward_kernel, 9, len(first)),
        grid=(seqs, KV_HEADS, 2),
        in_specs=[
            pl.BlockSpec((1, table.shape[1]), lambda s, g, h: (s, 0), memory_space=pltpu.SMEM),
            rows_spec,
            pl.BlockSpec((ranks, 1, rows, HEAD), lambda s, g, h: (0, s, 0, g)),
            pl.BlockSpec((ranks, 1, rows, HEAD), lambda s, g, h: (0, s, 0, KV_HEADS + g)),
            rows_spec,
            rows_spec,
            pl.BlockSpec((1, 1, 1, GROUP, block), lambda s, g, h: (s, g, h, 0, 0)),
            trig_spec,
            trig_spec,
            *(pl.BlockSpec(memory_space=pl.ANY) for _ in first),
        ],
        out_specs=[
            rows_spec,
            pl.BlockSpec((ranks, 1, 2, rows, HEAD), lambda s, g, h: (0, s, 0, 0, g)),
        ],
        out_shape=[
            jax.ShapeDtypeStruct(queries.shape, jnp.bfloat16),
            jax.ShapeDtypeStruct((ranks, seqs, 2, rows, KV_HEADS * HEAD), jnp.bfloat16),
        ],
        scratch_shapes=[
            pltpu.VMEM((ranks, rows, HEAD), jnp.float32),
            pltpu.VMEM((ranks, rows, HEAD), jnp.float32),
            pltpu.VMEM((GROUP, HEAD, block), jnp.float32),
            pltpu.VMEM((GROUP, 1, block), jnp.float32),
        ],
        compiler_params=pltpu.CompilerParams(vmem_limit_bytes=40 * MIB),
        cost_estimate=cost(
            10 * HEAD * work, 12 * MIB, work
        ),
        name="attend_backward",
    )(table, queries, kv, kv, grads, attended, lse, cosine, signed_sine, *first)


def grad_kernel(count, *refs):
    kept, sent = refs[-2:]
    total = None
    for left, right in zip(refs[:count], refs[count : 2 * count]):
        term = dot(left[...], right[...], NN)
        total = term if total is None else total + term
    total = total.astype(kept.dtype)
    first = pl.program_id(0) < pl.num_programs(0) // 2

    @pl.when(first)
    def _():
        kept[...] = total

    @pl.when(jnp.logical_not(first))
    def _():
        sent[...] = total


def unit_grads(lefts, rights, *first):
    units = lefts[0].shape[0]
    rows, width = rights[0].shape
    count = len(lefts)
    block = units // 4
    half = jax.ShapeDtypeStruct((units // 2, width), jnp.bfloat16)
    return pl.pallas_call(
        with_tokens(functools.partial(grad_kernel, count), 2 * count, len(first)),
        grid=(4,),
        in_specs=[pl.BlockSpec((block, rows), lambda i: (i, 0)) for _ in lefts]
        + [pl.BlockSpec((rows, width), lambda i: (0, 0)) for _ in rights]
        + [pl.BlockSpec(memory_space=pl.ANY) for _ in first],
        out_specs=[
            pl.BlockSpec((block, width), lambda i: (jnp.minimum(i, 1), 0)),
            pl.BlockSpec((block, width), lambda i: (jnp.maximum(i - 2, 0), 0)),
        ],
        out_shape=[half, half],
        compiler_params=pltpu.CompilerParams(vmem_limit_bytes=56 * MIB),
        cost_estimate=cost(
            2 * count * units * rows * width,
            2 * count * rows * (units + width),
            0,
        ),
        name="unit_grads",
    )(*lefts, *rights, *first)


def back_kernel(count, *refs):
    out = refs[-1]
    total = None
    for left, right in zip(refs[:count], refs[count : 2 * count]):
        term = dot(left[...], right[...], TN)
        total = term if total is None else total + term
    out[...] = total.astype(out.dtype)


def back_rows(lefts, rights, *first):
    units, width = rights[0].shape
    rows = lefts[0].shape[1]
    count = len(lefts)
    block = width // 3
    return pl.pallas_call(
        with_tokens(functools.partial(back_kernel, count), 2 * count, len(first)),
        grid=(width // block,),
        in_specs=[pl.BlockSpec((units, rows), lambda i: (0, 0))] * count
        + [pl.BlockSpec((units, block), lambda i: (0, i))] * count
        + [pl.BlockSpec(memory_space=pl.ANY) for _ in first],
        out_specs=pl.BlockSpec((rows, block), lambda i: (0, i)),
        out_shape=jax.ShapeDtypeStruct((rows, width), jnp.bfloat16),
        compiler_params=pltpu.CompilerParams(vmem_limit_bytes=56 * MIB),
        cost_estimate=cost(2 * count * units * rows * width, 2 * count * units * (rows + width)),
        name="back_rows",
    )(*lefts, *rights, *first)


def hidden_kernel(rows, weight, out):
    out[...] = dot(weight[...], rows[...], NT).astype(out.dtype)


def hidden_rows(rows, weight):
    units, width = weight.shape
    count = rows.shape[0]
    block = units // 4
    return pl.pallas_call(
        hidden_kernel,
        grid=(4,),
        in_specs=[
            pl.BlockSpec((count, width), lambda i: (0, 0)),
            pl.BlockSpec((block, width), lambda i: (i, 0)),
        ],
        out_specs=pl.BlockSpec((block, count), lambda i: (i, 0)),
        out_shape=jax.ShapeDtypeStruct((units, count), jnp.bfloat16),
        compiler_params=pltpu.CompilerParams(vmem_limit_bytes=32 * MIB),
        cost_estimate=cost(2 * units * count * width, 2 * units * (count + width)),
        name="hidden_rows",
    )(rows, weight)


def project_kernel(rows_ref, gain, weight, bias, cosine, signed_sine, normed, queries, kv):
    step = pl.program_id(0)
    query_steps = pl.num_programs(0) - 2

    @pl.when(step == 0)
    def _():
        rows = rows_ref[...].astype(jnp.float32)
        scale = lax.rsqrt(jnp.mean(rows * rows, axis=-1, keepdims=True) + norm_eps)
        normed[...] = (rows * scale * gain[...]).astype(normed.dtype)

    out = dot(normed[...], weight[...], NT) + bias[...]

    def turned():
        parts = []
        for start in range(0, out.shape[1], HEAD):
            part = out[:, start : start + HEAD]
            parts.append(part * cosine[...] + pltpu.roll(part, HEAD // 2, 1) * signed_sine[...])
        return jnp.concatenate(parts, axis=1).astype(queries.dtype)

    @pl.when(step < query_steps)
    def _():
        queries[...] = turned()

    @pl.when(step == query_steps)
    def _():
        kv[...] = turned()

    @pl.when(step > query_steps)
    def _():
        kv[...] = out.astype(kv.dtype)


def project_heads(tokens, gain, weight, bias, cosine, signed_sine, *first):
    rows, width = tokens.shape
    block = KV_HEADS * HEAD
    steps = weight.shape[0] // block
    whole = pl.BlockSpec((rows, width), lambda i: (0, 0))
    table = pl.BlockSpec((rows, HEAD), lambda i: (0, 0))
    low = jnp.bfloat16
    return pl.pallas_call(
        with_tokens(project_kernel, 6, len(first)),
        grid=(steps,),
        in_specs=[
            whole,
            pl.BlockSpec((1, width), lambda i: (0, 0)),
            pl.BlockSpec((block, width), lambda i: (i, 0)),
            pl.BlockSpec((1, block), lambda i: (0, i)),
            table,
            table,
            *(pl.BlockSpec(memory_space=pl.ANY) for _ in first),
        ],
        out_specs=[
            whole,
            pl.BlockSpec((rows, block), lambda i: (0, jnp.minimum(i, steps - 3))),
            pl.BlockSpec((rows, block), lambda i: (0, jnp.maximum(i - steps + 2, 0))),
        ],
        out_shape=[
            jax.ShapeDtypeStruct((rows, width), low),
            jax.ShapeDtypeStruct((rows, (steps - 2) * block), low),
            jax.ShapeDtypeStruct((rows, 2 * block), low),
        ],
        compiler_params=pltpu.CompilerParams(vmem_limit_bytes=40 * MIB),
        cost_estimate=cost(
            2 * rows * width * weight.shape[0],
            2 * (weight.size + 4 * tokens.size),
            0,
        ),
        name="project_heads",
    )(tokens, gain, weight, bias, cosine, signed_sine, *first)


def unit_kernel(normed, d_hidden, gate, up, hidden, d_gate, d_up):
    gate_pre = dot(gate[...], normed[...], NT)
    up_pre = dot(up[...], normed[...], NT)
    d_mid = d_hidden[...].astype(jnp.float32)
    sig = 1.0 / (1.0 + jnp.exp(-gate_pre))
    silu = gate_pre * sig
    hidden[...] = (silu * up_pre).astype(hidden.dtype)
    d_up[...] = (d_mid * silu).astype(d_up.dtype)
    d_gate[...] = (d_mid * up_pre * (sig + silu * (1.0 - sig))).astype(d_gate.dtype)


def unit_rows(normed, d_hidden, gate, up):
    units, width = gate.shape
    rows = normed.shape[0]
    block = units // 4
    part = pl.BlockSpec((block, width), lambda i: (i, 0))
    out = pl.BlockSpec((block, rows), lambda i: (i, 0))
    shape = jax.ShapeDtypeStruct((units, rows), jnp.bfloat16)
    return pl.pallas_call(
        unit_kernel,
        grid=(4,),
        in_specs=[pl.BlockSpec((rows, width), lambda i: (0, 0)), out, part, part],
        out_specs=[out, out, out],
        out_shape=[shape, shape, shape],
        compiler_params=pltpu.CompilerParams(vmem_limit_bytes=48 * MIB),
        cost_estimate=cost(
            4 * units * rows * width, 4 * units * width + 8 * units * rows, 2 * units * rows
        ),
        name="unit_rows",
    )(normed, d_hidden, gate, up)


def rope_tables(positions):
    exponent = jnp.arange(0, HEAD, 2).astype(jnp.float32) / HEAD
    inverse = rope_base ** (-exponent)
    angles = positions.astype(jnp.float32)[:, None] * inverse[None, :]
    angles = jnp.concatenate([angles, angles], axis=1)
    return (jnp.cos(angles), jnp.sin(angles))


def rms_scale(values):
    return lax.rsqrt(jnp.mean(values * values, axis=-1, keepdims=True) + norm_eps)


def norm_back(d_normed, values, inv_scale, gain):
    scaled = d_normed * gain
    grad_gain = jnp.sum(d_normed * values * inv_scale, axis=0)
    inner = jnp.mean(scaled * values, axis=-1, keepdims=True)
    return (inv_scale * scaled - values * inv_scale * inv_scale * inv_scale * inner, grad_gain)


def project_rows(left, weight_rows):
    return jnp.einsum("rd,fd->rf", left, weight_rows, preferred_element_type=jnp.float32)


def flip(values, axis):
    return lax.ppermute(values, axis, [(0, 1), (1, 0)])


ALL_AXES = ("fa", "fb", "fc", "ch", "cl")
CTX_AXES = ("ch", "cl")


def over_a(values):
    if lax.axis_size("fa") == 2:
        return flip(values, "fa")
    return lax.all_gather(values, "fa", axis=0, tiled=True)


def join_a(own, other):
    return jnp.concatenate([own, other], axis=0) if lax.axis_size("fa") == 2 else other


def halves(values):
    half = values.shape[0] // 2
    return values[:half], values[half:]


def add_low(*terms):
    return functools.reduce(jnp.add, (t.astype(jnp.float32) for t in terms)).astype(jnp.bfloat16)


def add_core(kept, received):
    return [add_low(*pair) for pair in zip(halves(kept), halves(received))]


def over_a_sums(sums):
    if lax.axis_size("fa") == 2:
        return flip(sums[1], "fa")
    return lax.psum_scatter(jnp.concatenate(sums, axis=0), "fa", scatter_dimension=0, tiled=True)


def add_a(sums, received):
    return add_low(sums[0], received) if lax.axis_size("fa") == 2 else received


def core_kernel(core, left, right, kept, sent):
    total = dot(left[...], right[...], TN).astype(kept.dtype)

    @pl.when(pl.program_id(1) == 0)
    def _():
        kept[...] = total

    @pl.when(pl.program_id(1) == 1)
    def _():
        sent[...] = total


def core_terms(left, right, block, *first):
    rows, columns = left.shape
    width = right.shape[1]
    count = columns // block // 2
    me = lax.axis_index("fc")
    if block % 128:
        terms = dot(left, right, TN).astype(jnp.bfloat16).reshape(count, 2, block, width)
        pick = lambda k: lax.dynamic_index_in_dim(terms, k, 1, keepdims=False)
        return pick(me).reshape(-1, width), pick(1 - me).reshape(-1, width)
    out = pl.BlockSpec((block, width), lambda i, k, core: (i, 0))
    half = jax.ShapeDtypeStruct((count * block, width), jnp.bfloat16)
    return pl.pallas_call(
        with_tokens(core_kernel, 3, len(first)),
        grid_spec=pltpu.PrefetchScalarGridSpec(
            num_scalar_prefetch=1,
            grid=(count, 2),
            in_specs=[
                pl.BlockSpec((rows, block), lambda i, k, core: (0, 2 * i + (core[0] + k) % 2)),
                pl.BlockSpec((rows, width), lambda i, k, core: (0, 0)),
                *(pl.BlockSpec(memory_space=pl.ANY) for _ in first),
            ],
            out_specs=[out, out],
        ),
        out_shape=[half, half],
        compiler_params=pltpu.CompilerParams(vmem_limit_bytes=32 * MIB),
        cost_estimate=cost(2 * rows * columns * width, 2 * (rows + columns) * width),
        name="core_terms",
    )(me[None].astype(jnp.int32), left, right, *first)


def scatter_far(far):
    half = far.shape[0] // 2
    return flip(far[:half], "fb"), flip(far[half:], "cl")


def scatter_near(over_x, over_z, from_x, from_z):
    half = over_x.shape[0] // 2
    low, wide = jnp.bfloat16, jnp.float32
    over_x, over_z, from_x, from_z = (v.astype(wide) for v in (over_x, over_z, from_x, from_z))
    send_z = jnp.concatenate([over_z[:half] + from_x, over_z[half:]], axis=0)
    send_x = jnp.concatenate([over_x[:half], over_x[half:] + from_z], axis=0)
    return send_x.astype(low), send_z.astype(low)


def pack_vectors(vectors, blocks):
    flat = jnp.concatenate([v.reshape(blocks, -1) for v in vectors], axis=1)
    lanes = -(-flat.shape[1] // 1024) * 128
    flat = jnp.pad(flat, ((0, 0), (0, 8 * lanes - flat.shape[1])))
    return flat.reshape(blocks, 8, lanes)


def unpack_vectors(packed, sizes):
    flat = packed.reshape(packed.shape[0], -1)
    out = []
    start = 0
    for size in sizes:
        out.append(flat[:, start : start + size].reshape(-1))
        start += size
    return out


def xor_send(values, bits):
    count = lax.axis_size(CTX_AXES)
    return lax.ppermute(values, CTX_AXES, [(i, i ^ bits) for i in range(count)])


def stack_in_order(own, other, axis, dim):
    later = lax.axis_index(axis) == 1
    return jnp.stack([jnp.where(later, other, own), jnp.where(later, own, other)], axis=dim)


def stack_axis(values, axis, dim):
    if lax.axis_size(axis) == 2:
        return stack_in_order(values, flip(values, axis), axis, dim)
    return lax.all_gather(values, axis, axis=dim, tiled=False)


def order_ctx(*rel):
    high, low = lax.axis_index("ch") == 1, lax.axis_index("cl") == 1
    shape = rel[0].shape
    rel = [jnp.where(low, rel[k ^ 1], rel[k]) for k in range(4)]
    rel = [jnp.where(high, rel[k ^ 2], rel[k]) for k in range(4)]
    return jnp.stack(rel).reshape(2, 2, *shape)


def stack_plane_first(over_z):
    if lax.axis_size("fa") != 2:
        return stack_axis(over_z, "fb", 0), None
    return flip(over_z, "fa"), flip(over_z, "fb")


def stack_plane(over_z, by_a, by_b, far_top, far_bottom):
    far = jnp.concatenate([far_top, far_bottom], axis=2)
    near = stack_in_order(over_z, by_b, "fb", 0)
    beyond = stack_in_order(by_a, far, "fb", 0)
    return stack_in_order(near, beyond, "fa", 0)


def exchange(values, axes):
    return lax.all_to_all(values, axes, split_axis=0, concat_axis=0, tiled=True)


def nothing_kernel(*refs):
    pass


def gate(values, *first):
    anywhere = pl.BlockSpec(memory_space=pl.ANY)
    return pl.pallas_call(
        nothing_kernel,
        in_specs=[anywhere] * (1 + len(first)),
        out_specs=anywhere,
        out_shape=jax.ShapeDtypeStruct(values.shape, values.dtype),
        input_output_aliases={0: 0},
        cost_estimate=pl.CostEstimate(flops=0, bytes_accessed=0, transcendentals=0),
        name="gate",
    )(values, *first)


def copy_kernel(source, target):
    target[...] = source[...]


def gate_copy(values, *first):
    rows, width = values.shape
    block = rows // 2 if rows % 32 == 0 else rows
    spec = pl.BlockSpec((block, width), lambda i: (i, 0))
    return pl.pallas_call(
        with_tokens(copy_kernel, 1, len(first)),
        grid=(rows // block,),
        in_specs=[spec, *(pl.BlockSpec(memory_space=pl.ANY) for _ in first)],
        out_specs=spec,
        out_shape=jax.ShapeDtypeStruct(values.shape, values.dtype),
        cost_estimate=pl.CostEstimate(flops=0, bytes_accessed=0, transcendentals=0),
        name="gate_copy",
    )(values, *first)


def wait_kernel(source, target):
    target[...] = jnp.zeros_like(target)


def wait(first):
    return pl.pallas_call(
        wait_kernel,
        in_specs=[pl.BlockSpec(memory_space=pl.ANY)],
        out_shape=jax.ShapeDtypeStruct((8, 128), jnp.float32),
        cost_estimate=cost(10**10, 10**7),
        name="wait",
    )(first)


def on_device(
    tokens, stretch_pairs, cotangent, w_qkv, b_qkv, w_out, norm_attn, norm_mlp, w_gate, w_up, w_down
):
    ctx_count = lax.axis_size(CTX_AXES)
    device_count = lax.axis_size(ALL_AXES)
    device_grid = tuple(lax.axis_size(axis) for axis in ALL_AXES)
    ctx_rank = lax.axis_index(CTX_AXES)
    seq_count = stretch_pairs.shape[0]
    row_count, width = tokens.shape
    local_len = row_count // seq_count
    half_len = local_len // 2
    seq_len = local_len * ctx_count
    query_width = HEADS * HEAD
    kv_width = KV_HEADS * HEAD
    low, wide = jnp.bfloat16, jnp.float32

    half_rows = row_count // 2

    own_pair = lax.dynamic_slice_in_dim(stretch_pairs, ctx_rank, 1, axis=1)
    blocks = jnp.arange(2 * ctx_count)
    block_pair = jnp.minimum(blocks, 2 * ctx_count - 1 - blocks)
    holder = jnp.argmax(stretch_pairs[:, None, :] == block_pair[None, :, None], axis=2)
    slots = 2 * holder + (blocks >= ctx_count)[None, :]
    table = jnp.concatenate(
        [own_pair, 2 * ctx_count - 1 - own_pair, slots.astype(jnp.int32)], axis=1
    )
    offsets = jnp.arange(local_len)
    positions = jnp.where(
        offsets < half_len,
        own_pair * half_len + offsets,
        (2 * ctx_count - 1 - own_pair) * half_len + offsets - half_len,
    )
    cosine, sine_table = rope_tables(positions.reshape(row_count))
    signed_sine = jnp.where(jnp.arange(HEAD) < HEAD // 2, -sine_table, sine_table)

    vectors = pack_vectors([b_qkv, norm_attn, norm_mlp], 1)
    vectors_all = exchange(
        jnp.broadcast_to(vectors, (device_count, *vectors.shape[1:])), ALL_AXES
    )
    qkv_parts = [xor_send(w_qkv, k) for k in (1, 2, 3)]
    down_a = over_a(w_down)
    qkv_parts[0] = gate(qkv_parts[0], wait(w_qkv), down_a)
    qkv_z = order_ctx(w_qkv, *qkv_parts)
    by_a, by_b = stack_plane_first(qkv_z)
    own_down = gate_copy(w_down, qkv_z)
    down_z = flip(own_down, "ch")
    vectors_all = gate(vectors_all, qkv_z)
    cot_z = flip(gate_copy(cotangent, qkv_z), "cl")
    by_a = gate(by_a, wait(qkv_z))
    if by_b is None:
        qkv_plane = stack_axis(by_a, "fa", 0)
    else:
        far_top = flip(by_a[:, :, : by_a.shape[2] // 2], "fb")
        far_bottom = flip(by_b[:, :, by_b.shape[2] // 2 :], "fa")
        far_top = gate(far_top, wait(by_a))
        qkv_plane = stack_plane(qkv_z, by_a, by_b, far_top, far_bottom)
    out_all = lax.all_gather(gate_copy(w_out, qkv_plane), ALL_AXES, axis=0, tiled=True)
    cot_x = flip(gate_copy(cotangent, qkv_plane), "fb")
    own_gate = gate_copy(w_gate, qkv_plane)
    gate_a = over_a(own_gate)
    qkv_other = gate(flip(qkv_plane, "fc"), wait(qkv_plane))
    qkv_all = stack_in_order(qkv_plane, qkv_other, "fc", 2).reshape(-1, width)
    bias_all, gain_one, gain_two = unpack_vectors(
        vectors_all, (b_qkv.shape[0], norm_attn.shape[0], norm_mlp.shape[0])
    )
    gain_one, gain_two = gain_one.astype(wide)[None], gain_two.astype(wide)[None]

    normed_one, queries, kv_low = project_heads(
        tokens, gain_one, qkv_all, bias_all.astype(wide)[None], cosine, signed_sine
    )
    kv_low = kv_low.reshape(1, seq_count, local_len, 2 * kv_width)
    kv_sent = jnp.broadcast_to(kv_low, (ctx_count, *kv_low.shape[1:]))
    kv_all = exchange(kv_sent, CTX_AXES)
    cot_z, down_z = gate(cot_z, kv_sent), gate(down_z, kv_sent)
    cot_far = flip(cot_z, "fb")
    down_az = over_a(down_z)
    own_up = gate_copy(w_up, kv_sent)
    up_a = over_a(own_up)
    cot_parts = [cotangent, cot_x, cot_z, cot_far]

    gate_z = flip(gate_copy(w_gate, kv_all), "ch")
    queries = queries.reshape(seq_count, local_len, query_width)
    attended, log_totals = attend_forward(
        table, queries, kv_all, wait(kv_low), cot_x, cot_far, down_az, gate_a, up_a
    )
    attended_rows = attended.reshape(row_count, query_width)

    def middle_rows(rows, weight, inputs, gain):
        middle = inputs.astype(wide) + jnp.dot(rows, weight, preferred_element_type=wide)
        scale = rms_scale(middle)
        return (middle * scale * gain).astype(low), middle, scale

    normed_two, middle, inv_two = middle_rows(attended_rows, out_all, tokens, gain_two)

    def join_units(own, by_z, by_a, by_az):
        if lax.axis_size("fa") == 2:
            return jnp.concatenate([own, by_z, by_a, by_az], axis=0)
        blocks = [block.reshape(-1, *own.shape) for block in (by_a, by_az)]
        return jnp.concatenate(blocks, axis=1).reshape(-1, width)

    def join_core(own, other):
        return jnp.concatenate([own, other], axis=0)

    normed_x, normed_z = flip(normed_two, "fb"), flip(normed_two, "cl")
    up_z = flip(gate_copy(w_up, attended), "ch")
    down_own = join_units(own_down, down_z, down_a, gate(down_az, normed_two))
    down_part = join_core(down_own, gate(flip(down_own, "fc"), wait(down_own)))
    d_hidden = [hidden_rows(cot, down_part) for cot in cot_parts]
    gate_z = gate(gate_z, d_hidden[0])
    gate_az = over_a(gate_z)
    normed_x, normed_z = gate(normed_x, *d_hidden), gate(normed_z, *d_hidden)
    far_top, far_bottom = flip(normed_z[:half_rows], "fb"), flip(normed_x[half_rows:], "cl")
    gate_own = join_units(own_gate, gate_z, gate_a, gate(gate_az, *d_hidden))
    up_z = gate(up_z, gate_own)
    up_az = over_a(up_z)
    gate_part = join_core(gate_own, gate(flip(gate_own, "fc"), wait(gate_own)))
    normed_far = join_core(gate(far_top, gate_part), far_bottom)
    up_own = join_units(own_up, up_z, up_a, gate(up_az, gate_part))
    up_part = join_core(up_own, gate(flip(up_own, "fc"), wait(up_own)))
    normed_parts = [normed_two, normed_x, normed_z, normed_far]
    hidden, d_gate, d_up = zip(
        *(unit_rows(n, d, gate_part, up_part) for n, d in zip(normed_parts, d_hidden))
    )

    def back_units(k, *first):
        return back_rows((d_gate[k], d_up[k]), (gate_part, up_part), *first)

    def branch_rows(k, *first):
        return back_rows((hidden[k],), (down_part,), *first)

    back_far = back_units(3)
    back_from = scatter_far(back_far)
    back_x = back_units(1, back_far)
    back_z = back_units(2, back_x)
    back_sent = scatter_near(back_x, back_z, gate(back_from[0], back_z), back_from[1])
    back_x, back_z = flip(back_sent[0], "fb"), flip(back_sent[1], "cl")
    down_kept, down_sent = unit_grads(hidden, cot_parts, *back_sent)
    down_sent = flip(down_sent, "fc")
    back_own = back_units(0, down_kept)
    down_sums = add_core(down_kept, gate(down_sent, back_own))
    down_from_a = over_a_sums(down_sums)

    def back_norm(own, by_x, by_z, middle, scale, gain, cotangent):
        d_normed = own.astype(wide) + by_x.astype(wide) + by_z.astype(wide)
        d_rows, grad_gain = norm_back(d_normed, middle, scale, gain)
        d_middle = cotangent.astype(wide) + d_rows
        return d_middle.astype(low), d_middle, grad_gain

    d_branch, d_middle, grad_gain_two = back_norm(back_own, back_x, back_z, middle, inv_two, gain_two, cotangent
    )
    d_attended = project_rows(d_branch, out_all).astype(low)
    d_queries, d_kv_parts = attend_backward(
        table,
        queries,
        kv_all,
        d_attended.reshape(seq_count, local_len, query_width),
        attended,
        log_totals,
        cosine,
        signed_sine,
        *down_sums,
    )
    d_queries = d_queries.reshape(row_count, query_width)
    d_kv_parts = exchange(d_kv_parts, CTX_AXES)

    def add_three(own, by_x, by_z, middle):
        return (middle + own.astype(wide) + by_x.astype(wide) + by_z.astype(wide)).astype(low)

    def add_wide(own, other):
        return own.astype(wide) + other.astype(wide)

    def split_terms(left, right, *first):
        return core_terms(left, right, ctx_count * w_qkv.shape[0], *first)

    gate_kept, gate_sent = unit_grads(d_gate, normed_parts, d_queries)
    gate_sent = flip(gate_sent, "fc")
    down_sums = add_a(down_sums, gate(down_from_a, gate_kept))
    down_z_sums = flip(halves(down_sums)[1], "ch")
    grad_out = lax.psum_scatter(
        back_rows((attended_rows,), (d_branch,), gate_kept),
        ALL_AXES,
        scatter_dimension=0,
        tiled=True,
    ).astype(wide)
    query_kept, query_sent = split_terms(d_queries, normed_one, down_sums)
    query_sent = flip(query_sent, "fc")
    up_kept, up_sent = unit_grads(d_up, normed_parts, query_kept)
    up_sent = flip(up_sent, "fc")
    query_sums = add_low(query_kept, gate(query_sent, up_kept))
    gate_sums = add_core(gate_kept, gate(gate_sent, up_kept))
    gate_from_a = over_a_sums(gate_sums)
    branch_far = branch_rows(3, query_sums, *gate_sums)
    branch_from = flip(branch_far, "fb")
    up_sums = add_core(up_kept, gate(up_sent, branch_far))
    up_from_a = over_a_sums(up_sums)
    branch_x = branch_rows(1, *up_sums)
    branch_z = branch_rows(2, branch_x)
    branch_x = flip(branch_x, "fb")
    branch_z = add_low(branch_z, gate(branch_from, branch_z))
    gate_sums = add_a(gate_sums, gate(gate_from_a, branch_z))
    gate_z_sums = flip(halves(gate_sums)[1], "ch")
    d_kv_parts = gate(d_kv_parts, gate_sums)
    branch_z = flip(branch_z, "cl")
    query_bias_local = jnp.sum(d_queries, axis=0, dtype=wide)

    def turn_back(parts):
        d_kv = jnp.sum(parts, axis=0, dtype=wide)
        d_keys, d_values = (d_kv[:, k].reshape(row_count, kv_width) for k in (0, 1))
        turned = []
        for start in range(0, kv_width, HEAD):
            part = d_keys[:, start : start + HEAD]
            turned.append(part * cosine - jnp.roll(part, HEAD // 2, 1) * signed_sine)
        return jnp.concatenate([*turned, d_values], axis=1).astype(low)

    d_kv = turn_back(d_kv_parts)
    kv_kept, kv_sent = split_terms(d_kv, normed_one)
    kv_sent = gate(flip(kv_sent, "fc"), wait(kv_kept))
    kv_bias_local = jnp.sum(d_kv, axis=0, dtype=wide)

    def back_projection(d_queries, d_kv, weight):
        return dot(d_queries, weight[:query_width], NN) + dot(d_kv, weight[query_width:], NN)

    def back_tokens(d_normed, tokens, gain, d_middle):
        inputs = tokens.astype(wide)
        d_rows, grad_gain = norm_back(d_normed, inputs, rms_scale(inputs), gain)
        return d_middle + d_rows, grad_gain

    def join_qkv(query_sums, kept, sent):
        sums = jnp.concatenate([query_sums, add_wide(kept, sent).astype(low)], axis=0)
        return sums.reshape(-1, ctx_count, *w_qkv.shape)

    def add_all(values):
        return jnp.sum(values, axis=0, dtype=wide)

    d_normed_one = back_projection(d_queries, d_kv, qkv_all)
    grad_tokens, grad_gain_one = back_tokens(d_normed_one, tokens, gain_one, d_middle)
    vector_grads = [query_bias_local, kv_bias_local, grad_gain_one, grad_gain_two]
    qkv_terms = join_qkv(query_sums, kv_kept, gate(kv_sent, grad_tokens))
    qkv_sums = exchange(qkv_terms, ("fa", "fb"))
    up_sums = add_a(up_sums, gate(up_from_a, qkv_terms))
    up_z_sums = flip(halves(up_sums)[1], "ch")
    grad_down = add_wide(halves(down_sums)[0], gate(down_z_sums, up_sums))
    branch_own = branch_rows(0, grad_down)
    layer_out = add_three(branch_own, gate(branch_x, branch_own), branch_z, middle)
    qkv_sums = add_all(gate(qkv_sums, layer_out)).astype(low)

    def pick(rank):
        return lax.dynamic_index_in_dim(qkv_sums, rank, 0, keepdims=False)

    qkv_own = pick(ctx_rank)
    qkv_from = [xor_send(pick(ctx_rank ^ k), k) for k in (1, 2, 3)]
    packed = gate(pack_vectors(vector_grads, device_count), qkv_own)
    vector_shares = exchange(packed, ALL_AXES)
    qkv_from[0] = gate(qkv_from[0], wait(qkv_own), vector_shares)


    grad_gate = add_wide(halves(gate_sums)[0], gate_z_sums)
    grad_qkv = functools.reduce(jnp.add, (part.astype(wide) for part in (qkv_own, *qkv_from)))
    grad_up = add_wide(halves(up_sums)[0], up_z_sums)
    grad_query_bias, grad_kv_bias, grad_norm_attn, grad_norm_mlp = unpack_vectors(
        jnp.sum(vector_shares, axis=0)[None], [v.shape[0] // device_count for v in vector_grads]
    )
    return (
        layer_out,
        grad_tokens,
        grad_qkv,
        grad_query_bias,
        grad_kv_bias,
        grad_out,
        grad_norm_attn,
        grad_norm_mlp,
        grad_gate,
        grad_up,
        grad_down,
    )


def solution(mesh):
    fsdp_count, ctx_count = mesh.shape["fsdp"], mesh.shape["ctx"]
    parts = (fsdp_count // 4, 2, 2, ctx_count // 2, 2)
    split_mesh = Mesh(mesh.devices.reshape(parts), ALL_AXES)
    rows, whole = P(ALL_AXES, None), P(ALL_AXES)
    return jax.shard_map(
        on_device,
        mesh=split_mesh,
        in_specs=(
            rows,
            P(("fa", "fb", "fc"), None),
            rows,
            rows,
            whole,
            rows,
            whole,
            whole,
            rows,
            rows,
            rows,
        ),
        out_specs=(rows, rows, rows, whole, whole, rows, whole, whole, rows, rows, rows),
        check_vma=False,
    )
```

```python
import functools

import jax
import jax.numpy as jnp
from jax import lax
from jax.experimental import pallas as pl
from jax.experimental.pallas import tpu as pltpu
from jax.sharding import Mesh
from jax.sharding import PartitionSpec as P

HEADS = 12
KV_HEADS = 2
HEAD = 128
GROUP = HEADS // KV_HEADS
MIB = 2**20
COST_FACTOR = 16


def cost(flops, nbytes, transcendentals=0):
    return pl.CostEstimate(
        flops=flops * COST_FACTOR,
        bytes_accessed=nbytes * COST_FACTOR,
        transcendentals=transcendentals * COST_FACTOR,
    )


rope_base = 1000000.0
norm_eps = 1e-06

LOG2E = 1.4426950408889634
SCALE = HEAD ** -0.5

NT = (((1,), (1,)), ((), ()))
NN = (((1,), (0,)), ((), ()))
TN = (((0,), (0,)), ((), ()))


def with_tokens(kernel, count, tokens):
    return lambda *refs: kernel(*refs[:count], *refs[count + tokens :])


def dot(left, right, dims):
    return lax.dot_general(left, right, dims, preferred_element_type=jnp.float32)


def forward_kernel(table, q_ref, k_ref, v_ref, o_ref, lse_ref, top, total, acc):
    half = pl.program_id(2)
    block = q_ref.shape[1]
    last = table[0, half]
    spot = table[0, 2 + last]
    heads = range(GROUP)

    def part(slot, masked, first):
        rows = pl.ds(pl.multiple_of(slot % 2 * block, block), block)
        keys, values = k_ref[slot // 2, 0, rows, :], v_ref[slot // 2, 0, rows, :]
        if not first:
            old_top = [top[j] for j in heads]
            old_total = [total[j] for j in heads]
        scores = [dot(keys, q_ref[0, :, pl.ds(j * HEAD, HEAD)], NT) for j in heads]
        if masked:
            key_at = lax.broadcasted_iota(jnp.int32, scores[0].shape, 0)
            query_at = lax.broadcasted_iota(jnp.int32, scores[0].shape, 1)
            scores = [jnp.where(key_at <= query_at, s, -1e30) for s in scores]
        tops = [jnp.max(s, axis=0, keepdims=True) * (SCALE * LOG2E) for s in scores]
        if not first:
            tops = [jnp.maximum(t, o) for t, o in zip(tops, old_top)]
        expon = [jnp.exp2(s * (SCALE * LOG2E) - t) for s, t in zip(scores, tops)]
        sums = [jnp.sum(e, axis=0, keepdims=True) for e in expon]
        added = [dot(values, e.astype(jnp.bfloat16), TN) for e in expon]
        for j in heads:
            if first:
                total[j] = sums[j]
                acc[j] = added[j]
            else:
                fade = jnp.exp2(old_top[j] - tops[j])
                total[j] = old_total[j] * fade + sums[j]
                acc[j] = acc[j] * fade + added[j]
            top[j] = tops[j]

    part(spot, True, True)

    def step(b, carry):
        part(table[0, 2 + b], False, False)
        return carry

    lax.fori_loop(0, last, step, 0)
    for j in heads:
        o_ref[0, :, pl.ds(j * HEAD, HEAD)] = (acc[j] / total[j]).T.astype(jnp.bfloat16)
        lse_ref[0, 0, 0, j] = (top[j] + jnp.log2(total[j]))[0]


def attend_forward(table, queries, kv, *first):
    seqs, rows, width = queries.shape
    block = rows // 2
    wide = GROUP * HEAD
    ranks = kv.shape[0]
    work = HEADS * rows * rows * ranks * seqs * 9 // 16
    return pl.pallas_call(
        with_tokens(forward_kernel, 4, len(first)),
        grid=(seqs, KV_HEADS, 2),
        in_specs=[
            pl.BlockSpec((1, table.shape[1]), lambda s, g, h: (s, 0), memory_space=pltpu.SMEM),
            pl.BlockSpec((1, block, wide), lambda s, g, h: (s, h, g)),
            pl.BlockSpec((ranks, 1, rows, HEAD), lambda s, g, h: (0, s, 0, g)),
            pl.BlockSpec((ranks, 1, rows, HEAD), lambda s, g, h: (0, s, 0, KV_HEADS + g)),
            *(pl.BlockSpec(memory_space=pl.ANY) for _ in first),
        ],
        out_specs=[
            pl.BlockSpec((1, block, wide), lambda s, g, h: (s, h, g)),
            pl.BlockSpec((1, 1, 1, GROUP, block), lambda s, g, h: (s, g, h, 0, 0)),
        ],
        out_shape=[
            jax.ShapeDtypeStruct(queries.shape, jnp.bfloat16),
            jax.ShapeDtypeStruct((seqs, KV_HEADS, 2, GROUP, block), jnp.float32),
        ],
        scratch_shapes=[
            pltpu.VMEM((GROUP, 1, block), jnp.float32),
            pltpu.VMEM((GROUP, 1, block), jnp.float32),
            pltpu.VMEM((GROUP, HEAD, block), jnp.float32),
        ],
        compiler_params=pltpu.CompilerParams(vmem_limit_bytes=40 * MIB),
        cost_estimate=cost(
            4 * HEAD * work, 6 * MIB, work
        ),
        name="attend_forward",
    )(table, queries, kv, kv, *first)


def backward_kernel(table, q_ref, k_ref, v_ref, g_ref, o_ref, lse_ref, cos_ref, sin_ref, dq_ref, dkv_ref, dk_acc, dv_acc, dq_acc, delta):
    half = pl.program_id(2)
    block = q_ref.shape[1]
    last = table[0, half]
    heads = range(GROUP)

    for j in heads:
        lanes = pl.ds(j * HEAD, HEAD)
        product = o_ref[0, :, lanes].astype(jnp.float32) * g_ref[0, :, lanes].astype(jnp.float32)
        delta[j] = jnp.sum(product.T, axis=0, keepdims=True)

    @pl.when(half == 0)
    def _():
        dk_acc[...] = jnp.zeros_like(dk_acc)
        dv_acc[...] = jnp.zeros_like(dv_acc)

    def part(slot, masked, first):
        rows = pl.ds(pl.multiple_of(slot % 2 * block, block), block)
        keys, values = k_ref[slot // 2, 0, rows, :], v_ref[slot // 2, 0, rows, :]
        lanes = [pl.ds(j * HEAD, HEAD) for j in heads]
        scores = [dot(keys, q_ref[0, :, lanes[j]], NT) for j in heads]
        d_probs = [dot(values, g_ref[0, :, lanes[j]], NT) for j in heads]
        probs = [
            jnp.exp2(scores[j] * (SCALE * LOG2E) - lse_ref[0, 0, 0, pl.ds(j, 1), :]) for j in heads
        ]
        if masked:
            key_at = lax.broadcasted_iota(jnp.int32, scores[0].shape, 0)
            query_at = lax.broadcasted_iota(jnp.int32, scores[0].shape, 1)
            probs = [jnp.where(key_at <= query_at, p, 0.0) for p in probs]
        d_scores = [(probs[j] * (d_probs[j] - delta[j])).astype(jnp.bfloat16) for j in heads]
        low = [p.astype(jnp.bfloat16) for p in probs]
        dv = sum(dot(low[j], g_ref[0, :, lanes[j]], NN) for j in heads)
        dk = sum(dot(d_scores[j], q_ref[0, :, lanes[j]], NN) for j in heads)
        dq = [dot(keys, d_scores[j], TN) for j in heads]
        for j in heads:
            if first:
                dq_acc[j] = dq[j]
            else:
                dq_acc[j] += dq[j]
        dk_acc[slot // 2, rows, :] += dk
        dv_acc[slot // 2, rows, :] += dv

    part(table[0, 2 + last], True, True)

    def step(b, carry):
        part(table[0, 2 + b], False, False)
        return carry

    lax.fori_loop(0, last, step, 0)
    for j in heads:
        grad = dq_acc[j].T * SCALE
        grad = grad * cos_ref[...] - pltpu.roll(grad, HEAD // 2, 1) * sin_ref[...]
        dq_ref[0, :, pl.ds(j * HEAD, HEAD)] = grad.astype(dq_ref.dtype)

    @pl.when(half == 1)
    def _():
        dkv_ref[:, 0, 0] = (dk_acc[...] * SCALE).astype(dkv_ref.dtype)
        dkv_ref[:, 0, 1] = dv_acc[...].astype(dkv_ref.dtype)


def attend_backward(table, queries, kv, grads, attended, lse, cosine, signed_sine, *first):
    seqs, rows, width = queries.shape
    block = rows // 2
    wide = GROUP * HEAD
    ranks = kv.shape[0]
    work = HEADS * rows * rows * ranks * seqs * 9 // 16
    rows_spec = pl.BlockSpec((1, block, wide), lambda s, g, h: (s, h, g))
    trig_spec = pl.BlockSpec((block, HEAD), lambda s, g, h: (2 * s + h, 0))
    return pl.pallas_call(
        with_tokens(backward_kernel, 9, len(first)),
        grid=(seqs, KV_HEADS, 2),
        in_specs=[
            pl.BlockSpec((1, table.shape[1]), lambda s, g, h: (s, 0), memory_space=pltpu.SMEM),
            rows_spec,
            pl.BlockSpec((ranks, 1, rows, HEAD), lambda s, g, h: (0, s, 0, g)),
            pl.BlockSpec((ranks, 1, rows, HEAD), lambda s, g, h: (0, s, 0, KV_HEADS + g)),
            rows_spec,
            rows_spec,
            pl.BlockSpec((1, 1, 1, GROUP, block), lambda s, g, h: (s, g, h, 0, 0)),
            trig_spec,
            trig_spec,
            *(pl.BlockSpec(memory_space=pl.ANY) for _ in first),
        ],
        out_specs=[
            rows_spec,
            pl.BlockSpec((ranks, 1, 2, rows, HEAD), lambda s, g, h: (0, s, 0, 0, g)),
        ],
        out_shape=[
            jax.ShapeDtypeStruct(queries.shape, jnp.bfloat16),
            jax.ShapeDtypeStruct((ranks, seqs, 2, rows, KV_HEADS * HEAD), jnp.bfloat16),
        ],
        scratch_shapes=[
            pltpu.VMEM((ranks, rows, HEAD), jnp.float32),
            pltpu.VMEM((ranks, rows, HEAD), jnp.float32),
            pltpu.VMEM((GROUP, HEAD, block), jnp.float32),
            pltpu.VMEM((GROUP, 1, block), jnp.float32),
        ],
        compiler_params=pltpu.CompilerParams(vmem_limit_bytes=40 * MIB),
        cost_estimate=cost(
            10 * HEAD * work, 12 * MIB, work
        ),
        name="attend_backward",
    )(table, queries, kv, kv, grads, attended, lse, cosine, signed_sine, *first)


def grad_kernel(count, *refs):
    kept, sent = refs[-2:]
    total = None
    for left, right in zip(refs[:count], refs[count : 2 * count]):
        term = dot(left[...], right[...], NN)
        total = term if total is None else total + term
    total = total.astype(kept.dtype)
    first = pl.program_id(0) < pl.num_programs(0) // 2

    @pl.when(first)
    def _():
        kept[...] = total

    @pl.when(jnp.logical_not(first))
    def _():
        sent[...] = total


def unit_grads(lefts, rights, *first):
    units = lefts[0].shape[0]
    rows, width = rights[0].shape
    count = len(lefts)
    block = units // 4
    half = jax.ShapeDtypeStruct((units // 2, width), jnp.bfloat16)
    return pl.pallas_call(
        with_tokens(functools.partial(grad_kernel, count), 2 * count, len(first)),
        grid=(4,),
        in_specs=[pl.BlockSpec((block, rows), lambda i: (i, 0)) for _ in lefts]
        + [pl.BlockSpec((rows, width), lambda i: (0, 0)) for _ in rights]
        + [pl.BlockSpec(memory_space=pl.ANY) for _ in first],
        out_specs=[
            pl.BlockSpec((block, width), lambda i: (jnp.minimum(i, 1), 0)),
            pl.BlockSpec((block, width), lambda i: (jnp.maximum(i - 2, 0), 0)),
        ],
        out_shape=[half, half],
        compiler_params=pltpu.CompilerParams(vmem_limit_bytes=56 * MIB),
        cost_estimate=cost(
            2 * count * units * rows * width,
            2 * count * rows * (units + width),
            0,
        ),
        name="unit_grads",
    )(*lefts, *rights, *first)


def back_kernel(count, *refs):
    out = refs[-1]
    total = None
    for left, right in zip(refs[:count], refs[count : 2 * count]):
        term = dot(left[...], right[...], TN)
        total = term if total is None else total + term
    out[...] = total.astype(out.dtype)


def back_rows(lefts, rights, *first):
    units, width = rights[0].shape
    rows = lefts[0].shape[1]
    count = len(lefts)
    block = width // 3
    return pl.pallas_call(
        with_tokens(functools.partial(back_kernel, count), 2 * count, len(first)),
        grid=(width // block,),
        in_specs=[pl.BlockSpec((units, rows), lambda i: (0, 0))] * count
        + [pl.BlockSpec((units, block), lambda i: (0, i))] * count
        + [pl.BlockSpec(memory_space=pl.ANY) for _ in first],
        out_specs=pl.BlockSpec((rows, block), lambda i: (0, i)),
        out_shape=jax.ShapeDtypeStruct((rows, width), jnp.bfloat16),
        compiler_params=pltpu.CompilerParams(vmem_limit_bytes=56 * MIB),
        cost_estimate=cost(2 * count * units * rows * width, 2 * count * units * (rows + width)),
        name="back_rows",
    )(*lefts, *rights, *first)


def hidden_kernel(rows, weight, out):
    out[...] = dot(weight[...], rows[...], NT).astype(out.dtype)


def hidden_rows(rows, weight):
    units, width = weight.shape
    count = rows.shape[0]
    block = units // 4
    return pl.pallas_call(
        hidden_kernel,
        grid=(4,),
        in_specs=[
            pl.BlockSpec((count, width), lambda i: (0, 0)),
            pl.BlockSpec((block, width), lambda i: (i, 0)),
        ],
        out_specs=pl.BlockSpec((block, count), lambda i: (i, 0)),
        out_shape=jax.ShapeDtypeStruct((units, count), jnp.bfloat16),
        compiler_params=pltpu.CompilerParams(vmem_limit_bytes=32 * MIB),
        cost_estimate=cost(2 * units * count * width, 2 * units * (count + width)),
        name="hidden_rows",
    )(rows, weight)


def project_kernel(rows_ref, gain, weight, bias, cosine, signed_sine, normed, queries, kv):
    step = pl.program_id(0)
    query_steps = pl.num_programs(0) - 2

    @pl.when(step == 0)
    def _():
        rows = rows_ref[...].astype(jnp.float32)
        scale = lax.rsqrt(jnp.mean(rows * rows, axis=-1, keepdims=True) + norm_eps)
        normed[...] = (rows * scale * gain[...]).astype(normed.dtype)

    out = dot(normed[...], weight[...], NT) + bias[...]

    def turned():
        parts = []
        for start in range(0, out.shape[1], HEAD):
            part = out[:, start : start + HEAD]
            parts.append(part * cosine[...] + pltpu.roll(part, HEAD // 2, 1) * signed_sine[...])
        return jnp.concatenate(parts, axis=1).astype(queries.dtype)

    @pl.when(step < query_steps)
    def _():
        queries[...] = turned()

    @pl.when(step == query_steps)
    def _():
        kv[...] = turned()

    @pl.when(step > query_steps)
    def _():
        kv[...] = out.astype(kv.dtype)


def project_heads(tokens, gain, weight, bias, cosine, signed_sine, *first):
    rows, width = tokens.shape
    block = KV_HEADS * HEAD
    steps = weight.shape[0] // block
    whole = pl.BlockSpec((rows, width), lambda i: (0, 0))
    table = pl.BlockSpec((rows, HEAD), lambda i: (0, 0))
    low = jnp.bfloat16
    return pl.pallas_call(
        with_tokens(project_kernel, 6, len(first)),
        grid=(steps,),
        in_specs=[
            whole,
            pl.BlockSpec((1, width), lambda i: (0, 0)),
            pl.BlockSpec((block, width), lambda i: (i, 0)),
            pl.BlockSpec((1, block), lambda i: (0, i)),
            table,
            table,
            *(pl.BlockSpec(memory_space=pl.ANY) for _ in first),
        ],
        out_specs=[
            whole,
            pl.BlockSpec((rows, block), lambda i: (0, jnp.minimum(i, steps - 3))),
            pl.BlockSpec((rows, block), lambda i: (0, jnp.maximum(i - steps + 2, 0))),
        ],
        out_shape=[
            jax.ShapeDtypeStruct((rows, width), low),
            jax.ShapeDtypeStruct((rows, (steps - 2) * block), low),
            jax.ShapeDtypeStruct((rows, 2 * block), low),
        ],
        compiler_params=pltpu.CompilerParams(vmem_limit_bytes=40 * MIB),
        cost_estimate=cost(
            2 * rows * width * weight.shape[0],
            2 * (weight.size + 4 * tokens.size),
            0,
        ),
        name="project_heads",
    )(tokens, gain, weight, bias, cosine, signed_sine, *first)


def unit_kernel(normed, d_hidden, gate, up, hidden, d_gate, d_up):
    gate_pre = dot(gate[...], normed[...], NT)
    up_pre = dot(up[...], normed[...], NT)
    d_mid = d_hidden[...].astype(jnp.float32)
    sig = 1.0 / (1.0 + jnp.exp(-gate_pre))
    silu = gate_pre * sig
    hidden[...] = (silu * up_pre).astype(hidden.dtype)
    d_up[...] = (d_mid * silu).astype(d_up.dtype)
    d_gate[...] = (d_mid * up_pre * (sig + silu * (1.0 - sig))).astype(d_gate.dtype)


def unit_rows(normed, d_hidden, gate, up):
    units, width = gate.shape
    rows = normed.shape[0]
    block = units // 4
    part = pl.BlockSpec((block, width), lambda i: (i, 0))
    out = pl.BlockSpec((block, rows), lambda i: (i, 0))
    shape = jax.ShapeDtypeStruct((units, rows), jnp.bfloat16)
    return pl.pallas_call(
        unit_kernel,
        grid=(4,),
        in_specs=[pl.BlockSpec((rows, width), lambda i: (0, 0)), out, part, part],
        out_specs=[out, out, out],
        out_shape=[shape, shape, shape],
        compiler_params=pltpu.CompilerParams(vmem_limit_bytes=60 * MIB),
        cost_estimate=cost(
            4 * units * rows * width, 4 * units * width + 8 * units * rows, 2 * units * rows
        ),
        name="unit_rows",
    )(normed, d_hidden, gate, up)


def rope_tables(positions):
    exponent = jnp.arange(0, HEAD, 2).astype(jnp.float32) / HEAD
    inverse = rope_base ** (-exponent)
    angles = positions.astype(jnp.float32)[:, None] * inverse[None, :]
    angles = jnp.concatenate([angles, angles], axis=1)
    return (jnp.cos(angles), jnp.sin(angles))


def rms_scale(values):
    return lax.rsqrt(jnp.mean(values * values, axis=-1, keepdims=True) + norm_eps)


def norm_back(d_normed, values, inv_scale, gain):
    scaled = d_normed * gain
    grad_gain = jnp.sum(d_normed * values * inv_scale, axis=0)
    inner = jnp.mean(scaled * values, axis=-1, keepdims=True)
    return (inv_scale * scaled - values * inv_scale * inv_scale * inv_scale * inner, grad_gain)


def project_rows(left, weight_rows):
    return jnp.einsum("rd,fd->rf", left, weight_rows, preferred_element_type=jnp.float32)


def flip(values, axis):
    return lax.ppermute(values, axis, [(0, 1), (1, 0)])


ALL_AXES = ("fa", "fb", "fc", "ch", "cl")
CTX_AXES = ("ch", "cl")


def over_a(values):
    if lax.axis_size("fa") == 2:
        return flip(values, "fa")
    return lax.all_gather(values, "fa", axis=0, tiled=True)


def join_a(own, other):
    return jnp.concatenate([own, other], axis=0) if lax.axis_size("fa") == 2 else other


def halves(values):
    half = values.shape[0] // 2
    return values[:half], values[half:]


def add_low(*terms):
    return functools.reduce(jnp.add, (t.astype(jnp.float32) for t in terms)).astype(jnp.bfloat16)


def add_core(kept, received):
    return [add_low(*pair) for pair in zip(halves(kept), halves(received))]


def over_a_sums(sums):
    if lax.axis_size("fa") == 2:
        return flip(sums[1], "fa")
    return lax.psum_scatter(jnp.concatenate(sums, axis=0), "fa", scatter_dimension=0, tiled=True)


def add_a(sums, received):
    return add_low(sums[0], received) if lax.axis_size("fa") == 2 else received


def core_kernel(core, left, right, kept, sent):
    total = dot(left[...], right[...], TN).astype(kept.dtype)

    @pl.when(pl.program_id(1) == 0)
    def _():
        kept[...] = total

    @pl.when(pl.program_id(1) == 1)
    def _():
        sent[...] = total


def core_terms(left, right, block, *first):
    rows, columns = left.shape
    width = right.shape[1]
    count = columns // block // 2
    me = lax.axis_index("fc")
    if block % 128:
        terms = dot(left, right, TN).astype(jnp.bfloat16).reshape(count, 2, block, width)
        pick = lambda k: lax.dynamic_index_in_dim(terms, k, 1, keepdims=False)
        return pick(me).reshape(-1, width), pick(1 - me).reshape(-1, width)
    out = pl.BlockSpec((block, width), lambda i, k, core: (i, 0))
    half = jax.ShapeDtypeStruct((count * block, width), jnp.bfloat16)
    return pl.pallas_call(
        with_tokens(core_kernel, 3, len(first)),
        grid_spec=pltpu.PrefetchScalarGridSpec(
            num_scalar_prefetch=1,
            grid=(count, 2),
            in_specs=[
                pl.BlockSpec((rows, block), lambda i, k, core: (0, 2 * i + (core[0] + k) % 2)),
                pl.BlockSpec((rows, width), lambda i, k, core: (0, 0)),
                *(pl.BlockSpec(memory_space=pl.ANY) for _ in first),
            ],
            out_specs=[out, out],
        ),
        out_shape=[half, half],
        compiler_params=pltpu.CompilerParams(vmem_limit_bytes=32 * MIB),
        cost_estimate=cost(2 * rows * columns * width, 2 * (rows + columns) * width),
        name="core_terms",
    )(me[None].astype(jnp.int32), left, right, *first)


def scatter_far(far):
    half = far.shape[0] // 2
    return flip(far[:half], "fb"), flip(far[half:], "cl")


def scatter_near(over_x, over_z, from_x, from_z):
    half = over_x.shape[0] // 2
    low, wide = jnp.bfloat16, jnp.float32
    over_x, over_z, from_x, from_z = (v.astype(wide) for v in (over_x, over_z, from_x, from_z))
    send_z = jnp.concatenate([over_z[:half] + from_x, over_z[half:]], axis=0)
    send_x = jnp.concatenate([over_x[:half], over_x[half:] + from_z], axis=0)
    return send_x.astype(low), send_z.astype(low)


def pack_vectors(vectors, blocks):
    flat = jnp.concatenate([v.reshape(blocks, -1) for v in vectors], axis=1)
    lanes = -(-flat.shape[1] // 1024) * 128
    flat = jnp.pad(flat, ((0, 0), (0, 8 * lanes - flat.shape[1])))
    return flat.reshape(blocks, 8, lanes)


def unpack_vectors(packed, sizes):
    flat = packed.reshape(packed.shape[0], -1)
    out = []
    start = 0
    for size in sizes:
        out.append(flat[:, start : start + size].reshape(-1))
        start += size
    return out


def xor_send(values, bits):
    count = lax.axis_size(CTX_AXES)
    return lax.ppermute(values, CTX_AXES, [(i, i ^ bits) for i in range(count)])


def stack_in_order(own, other, axis, dim):
    later = lax.axis_index(axis) == 1
    return jnp.stack([jnp.where(later, other, own), jnp.where(later, own, other)], axis=dim)


def stack_axis(values, axis, dim):
    if lax.axis_size(axis) == 2:
        return stack_in_order(values, flip(values, axis), axis, dim)
    return lax.all_gather(values, axis, axis=dim, tiled=False)


def order_ctx(*rel):
    high, low = lax.axis_index("ch") == 1, lax.axis_index("cl") == 1
    shape = rel[0].shape
    rel = [jnp.where(low, rel[k ^ 1], rel[k]) for k in range(4)]
    rel = [jnp.where(high, rel[k ^ 2], rel[k]) for k in range(4)]
    return jnp.stack(rel).reshape(2, 2, *shape)


def stack_plane_first(over_z):
    if lax.axis_size("fa") != 2:
        return stack_axis(over_z, "fb", 0), None
    return flip(over_z, "fa"), flip(over_z, "fb")


def stack_plane(over_z, by_a, by_b, far_top, far_bottom):
    far = jnp.concatenate([far_top, far_bottom], axis=2)
    near = stack_in_order(over_z, by_b, "fb", 0)
    beyond = stack_in_order(by_a, far, "fb", 0)
    return stack_in_order(near, beyond, "fa", 0)


def exchange(values, axes):
    return lax.all_to_all(values, axes, split_axis=0, concat_axis=0, tiled=True)


def nothing_kernel(*refs):
    pass


def gate(values, *first):
    anywhere = pl.BlockSpec(memory_space=pl.ANY)
    return pl.pallas_call(
        nothing_kernel,
        in_specs=[anywhere] * (1 + len(first)),
        out_specs=anywhere,
        out_shape=jax.ShapeDtypeStruct(values.shape, values.dtype),
        input_output_aliases={0: 0},
        cost_estimate=pl.CostEstimate(flops=0, bytes_accessed=0, transcendentals=0),
        name="gate",
    )(values, *first)


def copy_kernel(source, target):
    target[...] = source[...]


def gate_copy(values, *first):
    rows, width = values.shape
    block = rows // 2 if rows % 32 == 0 else rows
    spec = pl.BlockSpec((block, width), lambda i: (i, 0))
    return pl.pallas_call(
        with_tokens(copy_kernel, 1, len(first)),
        grid=(rows // block,),
        in_specs=[spec, *(pl.BlockSpec(memory_space=pl.ANY) for _ in first)],
        out_specs=spec,
        out_shape=jax.ShapeDtypeStruct(values.shape, values.dtype),
        cost_estimate=pl.CostEstimate(flops=0, bytes_accessed=0, transcendentals=0),
        name="gate_copy",
    )(values, *first)


def wait_kernel(source, target):
    target[...] = jnp.zeros_like(target)


def wait(first):
    return pl.pallas_call(
        wait_kernel,
        in_specs=[pl.BlockSpec(memory_space=pl.ANY)],
        out_shape=jax.ShapeDtypeStruct((8, 128), jnp.float32),
        cost_estimate=cost(10**10, 10**7),
        name="wait",
    )(first)


def on_device(
    tokens, stretch_pairs, cotangent, w_qkv, b_qkv, w_out, norm_attn, norm_mlp, w_gate, w_up, w_down
):
    ctx_count = lax.axis_size(CTX_AXES)
    device_count = lax.axis_size(ALL_AXES)
    device_grid = tuple(lax.axis_size(axis) for axis in ALL_AXES)
    ctx_rank = lax.axis_index(CTX_AXES)
    seq_count = stretch_pairs.shape[0]
    row_count, width = tokens.shape
    local_len = row_count // seq_count
    half_len = local_len // 2
    seq_len = local_len * ctx_count
    query_width = HEADS * HEAD
    kv_width = KV_HEADS * HEAD
    low, wide = jnp.bfloat16, jnp.float32

    half_rows = row_count // 2

    own_pair = lax.dynamic_slice_in_dim(stretch_pairs, ctx_rank, 1, axis=1)
    blocks = jnp.arange(2 * ctx_count)
    block_pair = jnp.minimum(blocks, 2 * ctx_count - 1 - blocks)
    holder = jnp.argmax(stretch_pairs[:, None, :] == block_pair[None, :, None], axis=2)
    slots = 2 * holder + (blocks >= ctx_count)[None, :]
    table = jnp.concatenate(
        [own_pair, 2 * ctx_count - 1 - own_pair, slots.astype(jnp.int32)], axis=1
    )
    offsets = jnp.arange(local_len)
    positions = jnp.where(
        offsets < half_len,
        own_pair * half_len + offsets,
        (2 * ctx_count - 1 - own_pair) * half_len + offsets - half_len,
    )
    cosine, sine_table = rope_tables(positions.reshape(row_count))
    signed_sine = jnp.where(jnp.arange(HEAD) < HEAD // 2, -sine_table, sine_table)

    vectors = pack_vectors([b_qkv, norm_attn, norm_mlp], 1)
    vectors_all = exchange(
        jnp.broadcast_to(vectors, (device_count, *vectors.shape[1:])), ALL_AXES
    )
    qkv_parts = [xor_send(w_qkv, k) for k in (1, 2, 3)]
    down_a = over_a(w_down)
    qkv_parts[0] = gate(qkv_parts[0], wait(w_qkv))
    qkv_z = order_ctx(w_qkv, *qkv_parts)
    by_a, by_b = stack_plane_first(qkv_z)
    own_down = gate_copy(w_down, qkv_z)
    down_z = flip(own_down, "ch")
    vectors_all = gate(vectors_all, qkv_z)
    cot_z = flip(gate_copy(cotangent, qkv_z), "cl")
    by_a = gate(by_a, wait(qkv_z), down_a)
    if by_b is None:
        qkv_plane = stack_axis(by_a, "fa", 0)
    else:
        far_top = flip(by_a[:, :, : by_a.shape[2] // 2], "fb")
        far_bottom = flip(by_b[:, :, by_b.shape[2] // 2 :], "fa")
        far_top = gate(far_top, wait(by_a))
        qkv_plane = stack_plane(qkv_z, by_a, by_b, far_top, far_bottom)
    out_all = lax.all_gather(gate_copy(w_out, qkv_plane), ALL_AXES, axis=0, tiled=True)
    cot_x = flip(gate_copy(cotangent, qkv_plane), "fb")
    own_gate = gate_copy(w_gate, qkv_plane)
    gate_a = over_a(own_gate)
    qkv_other = gate(flip(qkv_plane, "fc"), wait(qkv_plane))
    qkv_all = stack_in_order(qkv_plane, qkv_other, "fc", 2).reshape(-1, width)
    bias_all, gain_one, gain_two = unpack_vectors(
        vectors_all, (b_qkv.shape[0], norm_attn.shape[0], norm_mlp.shape[0])
    )
    gain_one, gain_two = gain_one.astype(wide)[None], gain_two.astype(wide)[None]

    normed_one, queries, kv_low = project_heads(
        tokens, gain_one, qkv_all, bias_all.astype(wide)[None], cosine, signed_sine
    )
    kv_low = kv_low.reshape(1, seq_count, local_len, 2 * kv_width)
    kv_sent = jnp.broadcast_to(kv_low, (ctx_count, *kv_low.shape[1:]))
    kv_all = exchange(kv_sent, CTX_AXES)
    cot_z, down_z = gate(cot_z, kv_sent), gate(down_z, kv_sent)
    cot_far = flip(cot_z, "fb")
    down_az = over_a(down_z)
    own_up = gate_copy(w_up, kv_sent)
    up_a = over_a(own_up)
    cot_parts = [cotangent, cot_x, cot_z, cot_far]

    gate_z = flip(gate_copy(w_gate, kv_all), "ch")
    queries = queries.reshape(seq_count, local_len, query_width)
    attended, log_totals = attend_forward(
        table, queries, kv_all, wait(kv_low), cot_x, cot_far, down_az, gate_a, up_a
    )
    attended_rows = attended.reshape(row_count, query_width)

    def middle_rows(rows, weight, inputs, gain):
        middle = inputs.astype(wide) + jnp.dot(rows, weight, preferred_element_type=wide)
        scale = rms_scale(middle)
        return (middle * scale * gain).astype(low), middle, scale

    normed_two, middle, inv_two = middle_rows(attended_rows, out_all, tokens, gain_two)

    def join_units(own, by_z, by_a, by_az):
        if lax.axis_size("fa") == 2:
            return jnp.concatenate([own, by_z, by_a, by_az], axis=0)
        blocks = [block.reshape(-1, *own.shape) for block in (by_a, by_az)]
        return jnp.concatenate(blocks, axis=1).reshape(-1, width)

    def join_core(own, other):
        return jnp.concatenate([own, other], axis=0)

    normed_x, normed_z = flip(normed_two, "fb"), flip(normed_two, "cl")
    up_z = flip(gate_copy(w_up, attended), "ch")
    down_own = join_units(own_down, down_z, down_a, gate(down_az, normed_two))
    down_part = join_core(down_own, gate(flip(down_own, "fc"), wait(down_own)))
    d_hidden = [hidden_rows(cot, down_part) for cot in cot_parts]
    gate_z = gate(gate_z, d_hidden[0])
    gate_az = over_a(gate_z)
    normed_x, normed_z = gate(normed_x, *d_hidden), gate(normed_z, *d_hidden)
    far_top, far_bottom = flip(normed_z[:half_rows], "fb"), flip(normed_x[half_rows:], "cl")
    gate_own = join_units(own_gate, gate_z, gate_a, gate(gate_az, *d_hidden))
    up_z = gate(up_z, gate_own)
    up_az = over_a(up_z)
    gate_part = join_core(gate_own, gate(flip(gate_own, "fc"), wait(gate_own)))
    normed_far = join_core(gate(far_top, gate_part), far_bottom)
    up_own = join_units(own_up, up_z, up_a, gate(up_az, gate_part))
    up_part = join_core(up_own, gate(flip(up_own, "fc"), wait(up_own)))
    normed_parts = [normed_two, normed_x, normed_z, normed_far]
    hidden, d_gate, d_up = zip(
        *(unit_rows(n, d, gate_part, up_part) for n, d in zip(normed_parts, d_hidden))
    )

    def back_units(k, *first):
        return back_rows((d_gate[k], d_up[k]), (gate_part, up_part), *first)

    def branch_rows(k, *first):
        return back_rows((hidden[k],), (down_part,), *first)

    back_far = back_units(3)
    back_from = scatter_far(back_far)
    back_x = back_units(1, back_far)
    back_z = back_units(2, back_x)
    back_sent = scatter_near(back_x, back_z, gate(back_from[0], back_z), back_from[1])
    back_x, back_z = flip(back_sent[0], "fb"), flip(back_sent[1], "cl")
    down_kept, down_sent = unit_grads(hidden, cot_parts, *back_sent)
    down_sent = flip(down_sent, "fc")
    back_own = back_units(0, down_kept)
    down_sums = add_core(down_kept, gate(down_sent, back_own))
    down_from_a = over_a_sums(down_sums)

    def back_norm(own, by_x, by_z, middle, scale, gain, cotangent):
        d_normed = own.astype(wide) + by_x.astype(wide) + by_z.astype(wide)
        d_rows, grad_gain = norm_back(d_normed, middle, scale, gain)
        d_middle = cotangent.astype(wide) + d_rows
        return d_middle.astype(low), d_middle, grad_gain

    d_branch, d_middle, grad_gain_two = back_norm(back_own, back_x, back_z, middle, inv_two, gain_two, cotangent
    )
    d_attended = project_rows(d_branch, out_all).astype(low)
    d_queries, d_kv_parts = attend_backward(
        table,
        queries,
        kv_all,
        d_attended.reshape(seq_count, local_len, query_width),
        attended,
        log_totals,
        cosine,
        signed_sine,
        *down_sums,
    )
    d_queries = d_queries.reshape(row_count, query_width)
    d_kv_parts = exchange(d_kv_parts, CTX_AXES)

    def add_wide(own, other):
        return own.astype(wide) + other.astype(wide)

    def split_terms(left, right, *first):
        return core_terms(left, right, ctx_count * w_qkv.shape[0], *first)

    def turn_back(parts):
        d_kv = jnp.sum(parts, axis=0, dtype=wide)
        d_keys, d_values = (d_kv[:, k].reshape(row_count, kv_width) for k in (0, 1))
        turned = []
        for start in range(0, kv_width, HEAD):
            part = d_keys[:, start : start + HEAD]
            turned.append(part * cosine - jnp.roll(part, HEAD // 2, 1) * signed_sine)
        return jnp.concatenate([*turned, d_values], axis=1).astype(low)

    gate_kept, gate_sent = unit_grads(d_gate, normed_parts, d_queries)
    gate_sent = flip(gate_sent, "fc")
    grad_out_local = back_rows((attended_rows,), (d_branch,), gate_kept)
    grad_out = lax.psum_scatter(grad_out_local, ALL_AXES, scatter_dimension=0, tiled=True)
    down_sums = add_a(down_sums, gate(down_from_a, grad_out_local))
    down_z_sums = flip(halves(down_sums)[1], "ch")
    query_kept, query_sent = split_terms(d_queries, normed_one, down_sums)
    query_sent = flip(query_sent, "fc")
    gate_sums = add_core(gate_kept, gate(gate_sent, query_kept))
    gate_from_a = over_a_sums(gate_sums)
    up_kept, up_sent = unit_grads(d_up, normed_parts, *gate_sums)
    up_sent = flip(up_sent, "fc")
    branch_far = branch_rows(3, up_kept)
    branch_from = flip(branch_far, "fb")
    branch_z = branch_rows(2, branch_far)
    d_kv = turn_back(gate(d_kv_parts, branch_z))
    query_sums = add_low(query_kept, gate(query_sent, d_kv))
    gate_sums = add_a(gate_sums, gate(gate_from_a, query_sums))
    gate_z_sums = flip(halves(gate_sums)[1], "ch")
    up_sums = add_core(up_kept, gate(up_sent, gate_sums))
    up_from_a = over_a_sums(up_sums)
    kv_kept, kv_sent = split_terms(d_kv, normed_one, *up_sums)
    kv_sent = flip(kv_sent, "fc")
    query_bias_local = jnp.sum(d_queries, axis=0, dtype=wide)
    kv_bias_local = jnp.sum(d_kv, axis=0, dtype=wide)

    def back_projection(d_queries, d_kv, weight):
        return dot(d_queries, weight[:query_width], NN) + dot(d_kv, weight[query_width:], NN)

    def back_tokens(d_normed, tokens, gain, d_middle):
        inputs = tokens.astype(wide)
        d_rows, grad_gain = norm_back(d_normed, inputs, rms_scale(inputs), gain)
        return d_middle + d_rows, grad_gain

    def join_qkv(query_sums, kept, sent):
        sums = jnp.concatenate([query_sums, add_wide(kept, sent).astype(low)], axis=0)
        return sums.reshape(-1, ctx_count, *w_qkv.shape)

    def add_all(values):
        return jnp.sum(values, axis=0, dtype=wide)

    qkv_terms = join_qkv(query_sums, kv_kept, gate(kv_sent, wait(kv_kept)))
    qkv_sums = exchange(qkv_terms, ("fa", "fb"))
    d_normed_one = back_projection(d_queries, gate(d_kv, qkv_terms), qkv_all)
    grad_tokens, grad_gain_one = back_tokens(d_normed_one, tokens, gain_one, d_middle)
    vector_grads = [query_bias_local, kv_bias_local, grad_gain_one, grad_gain_two]
    branch_x = branch_rows(1, grad_tokens)
    branch_own = branch_rows(0, branch_x)
    branch_x = flip(branch_x, "fb")
    branch_z = add_low(branch_z, gate(branch_from, branch_own))
    grad_down = add_wide(halves(down_sums)[0], gate(down_z_sums, branch_z))
    branch_z = flip(branch_z, "cl")
    up_sums = add_a(up_sums, gate(up_from_a, grad_down))
    up_z_sums = flip(halves(up_sums)[1], "ch")
    grad_gate = add_wide(halves(gate_sums)[0], gate(gate_z_sums, up_sums))
    qkv_sums = add_all(gate(qkv_sums, grad_gate)).astype(low)
    branch_sum = add_wide(branch_own, gate(branch_x, qkv_sums))
    qkv_sums = gate(qkv_sums, branch_sum)

    def pick(rank):
        return lax.dynamic_index_in_dim(qkv_sums, rank, 0, keepdims=False)

    qkv_own = pick(ctx_rank)
    qkv_from = [xor_send(pick(ctx_rank ^ k), k) for k in (1, 2, 3)]
    packed = gate(pack_vectors(vector_grads, device_count), pick(ctx_rank ^ 3))
    vector_shares = exchange(packed, ALL_AXES)
    branch_z = gate(branch_z, pick(ctx_rank ^ 2))
    layer_out = (middle + add_wide(branch_z, branch_sum)).astype(low)
    qkv_from[0] = gate(qkv_from[0], wait(qkv_own), layer_out)
    grad_out = gate(grad_out, qkv_own).astype(wide)
    grad_qkv = functools.reduce(jnp.add, (part.astype(wide) for part in (qkv_own, *qkv_from)))
    grad_up = add_wide(halves(up_sums)[0], gate(up_z_sums, grad_qkv))
    grad_query_bias, grad_kv_bias, grad_norm_attn, grad_norm_mlp = unpack_vectors(
        jnp.sum(vector_shares, axis=0)[None], [v.shape[0] // device_count for v in vector_grads]
    )
    return (
        layer_out,
        grad_tokens,
        grad_qkv,
        grad_query_bias,
        grad_kv_bias,
        grad_out,
        grad_norm_attn,
        grad_norm_mlp,
        grad_gate,
        grad_up,
        grad_down,
    )


def solution(mesh):
    fsdp_count, ctx_count = mesh.shape["fsdp"], mesh.shape["ctx"]
    parts = (fsdp_count // 4, 2, 2, ctx_count // 2, 2)
    split_mesh = Mesh(mesh.devices.reshape(parts), ALL_AXES)
    rows, whole = P(ALL_AXES, None), P(ALL_AXES)
    return jax.shard_map(
        on_device,
        mesh=split_mesh,
        in_specs=(
            rows,
            P(("fa", "fb", "fc"), None),
            rows,
            rows,
            whole,
            rows,
            whole,
            whole,
            rows,
            rows,
            rows,
        ),
        out_specs=(rows, rows, rows, whole, whole, rows, whole, whole, rows, rows, rows),
        check_vma=False,
    )
```

```python
import functools

import jax
import jax.numpy as jnp
from jax import lax
from jax.experimental import pallas as pl
from jax.experimental.pallas import tpu as pltpu
from jax.sharding import Mesh
from jax.sharding import PartitionSpec as P

HEADS = 12
KV_HEADS = 2
HEAD = 128
GROUP = HEADS // KV_HEADS
MIB = 2**20
COST_FACTOR = 16


def cost(flops, nbytes, transcendentals=0):
    return pl.CostEstimate(
        flops=flops * COST_FACTOR,
        bytes_accessed=nbytes * COST_FACTOR,
        transcendentals=transcendentals * COST_FACTOR,
    )


rope_base = 1000000.0
norm_eps = 1e-06

LOG2E = 1.4426950408889634
SCALE = HEAD ** -0.5

NT = (((1,), (1,)), ((), ()))
NN = (((1,), (0,)), ((), ()))
TN = (((0,), (0,)), ((), ()))


def with_tokens(kernel, count, tokens):
    return lambda *refs: kernel(*refs[:count], *refs[count + tokens :])


def dot(left, right, dims):
    return lax.dot_general(left, right, dims, preferred_element_type=jnp.float32)


def forward_kernel(table, q_ref, k_ref, v_ref, o_ref, lse_ref, top, total, acc):
    half = pl.program_id(2)
    block = q_ref.shape[1]
    last = table[0, half]
    spot = table[0, 2 + last]
    heads = range(GROUP)

    def part(slot, masked, first):
        rows = pl.ds(pl.multiple_of(slot % 2 * block, block), block)
        keys, values = k_ref[slot // 2, 0, rows, :], v_ref[slot // 2, 0, rows, :]
        if not first:
            old_top = [top[j] for j in heads]
            old_total = [total[j] for j in heads]
        scores = [dot(keys, q_ref[0, :, pl.ds(j * HEAD, HEAD)], NT) for j in heads]
        if masked:
            key_at = lax.broadcasted_iota(jnp.int32, scores[0].shape, 0)
            query_at = lax.broadcasted_iota(jnp.int32, scores[0].shape, 1)
            scores = [jnp.where(key_at <= query_at, s, -1e30) for s in scores]
        tops = [jnp.max(s, axis=0, keepdims=True) * (SCALE * LOG2E) for s in scores]
        if not first:
            tops = [jnp.maximum(t, o) for t, o in zip(tops, old_top)]
        expon = [jnp.exp2(s * (SCALE * LOG2E) - t) for s, t in zip(scores, tops)]
        sums = [jnp.sum(e, axis=0, keepdims=True) for e in expon]
        added = [dot(values, e.astype(jnp.bfloat16), TN) for e in expon]
        for j in heads:
            if first:
                total[j] = sums[j]
                acc[j] = added[j]
            else:
                fade = jnp.exp2(old_top[j] - tops[j])
                total[j] = old_total[j] * fade + sums[j]
                acc[j] = acc[j] * fade + added[j]
            top[j] = tops[j]

    part(spot, True, True)

    def step(b, carry):
        part(table[0, 2 + b], False, False)
        return carry

    lax.fori_loop(0, last, step, 0)
    for j in heads:
        o_ref[0, :, pl.ds(j * HEAD, HEAD)] = (acc[j] / total[j]).T.astype(jnp.bfloat16)
        lse_ref[0, 0, 0, j] = (top[j] + jnp.log2(total[j]))[0]


def attend_forward(table, queries, kv, *first):
    seqs, rows, width = queries.shape
    block = rows // 2
    wide = GROUP * HEAD
    ranks = kv.shape[0]
    work = HEADS * rows * rows * ranks * seqs * 9 // 16
    return pl.pallas_call(
        with_tokens(forward_kernel, 4, len(first)),
        grid=(seqs, KV_HEADS, 2),
        in_specs=[
            pl.BlockSpec((1, table.shape[1]), lambda s, g, h: (s, 0), memory_space=pltpu.SMEM),
            pl.BlockSpec((1, block, wide), lambda s, g, h: (s, h, g)),
            pl.BlockSpec((ranks, 1, rows, HEAD), lambda s, g, h: (0, s, 0, g)),
            pl.BlockSpec((ranks, 1, rows, HEAD), lambda s, g, h: (0, s, 0, KV_HEADS + g)),
            *(pl.BlockSpec(memory_space=pl.ANY) for _ in first),
        ],
        out_specs=[
            pl.BlockSpec((1, block, wide), lambda s, g, h: (s, h, g)),
            pl.BlockSpec((1, 1, 1, GROUP, block), lambda s, g, h: (s, g, h, 0, 0)),
        ],
        out_shape=[
            jax.ShapeDtypeStruct(queries.shape, jnp.bfloat16),
            jax.ShapeDtypeStruct((seqs, KV_HEADS, 2, GROUP, block), jnp.float32),
        ],
        scratch_shapes=[
            pltpu.VMEM((GROUP, 1, block), jnp.float32),
            pltpu.VMEM((GROUP, 1, block), jnp.float32),
            pltpu.VMEM((GROUP, HEAD, block), jnp.float32),
        ],
        compiler_params=pltpu.CompilerParams(vmem_limit_bytes=40 * MIB),
        cost_estimate=cost(
            4 * HEAD * work, 6 * MIB, work
        ),
        name="attend_forward",
    )(table, queries, kv, kv, *first)


def backward_kernel(table, q_ref, k_ref, v_ref, g_ref, o_ref, lse_ref, cos_ref, sin_ref, dq_ref, dkv_ref, dk_acc, dv_acc, dq_acc, delta):
    half = pl.program_id(2)
    block = q_ref.shape[1]
    last = table[0, half]
    heads = range(GROUP)

    for j in heads:
        lanes = pl.ds(j * HEAD, HEAD)
        product = o_ref[0, :, lanes].astype(jnp.float32) * g_ref[0, :, lanes].astype(jnp.float32)
        delta[j] = jnp.sum(product.T, axis=0, keepdims=True)

    @pl.when(half == 0)
    def _():
        dk_acc[...] = jnp.zeros_like(dk_acc)
        dv_acc[...] = jnp.zeros_like(dv_acc)

    def part(slot, masked, first):
        rows = pl.ds(pl.multiple_of(slot % 2 * block, block), block)
        keys, values = k_ref[slot // 2, 0, rows, :], v_ref[slot // 2, 0, rows, :]
        lanes = [pl.ds(j * HEAD, HEAD) for j in heads]
        scores = [dot(keys, q_ref[0, :, lanes[j]], NT) for j in heads]
        d_probs = [dot(values, g_ref[0, :, lanes[j]], NT) for j in heads]
        probs = [
            jnp.exp2(scores[j] * (SCALE * LOG2E) - lse_ref[0, 0, 0, pl.ds(j, 1), :]) for j in heads
        ]
        if masked:
            key_at = lax.broadcasted_iota(jnp.int32, scores[0].shape, 0)
            query_at = lax.broadcasted_iota(jnp.int32, scores[0].shape, 1)
            probs = [jnp.where(key_at <= query_at, p, 0.0) for p in probs]
        d_scores = [(probs[j] * (d_probs[j] - delta[j])).astype(jnp.bfloat16) for j in heads]
        low = [p.astype(jnp.bfloat16) for p in probs]
        dv = sum(dot(low[j], g_ref[0, :, lanes[j]], NN) for j in heads)
        dk = sum(dot(d_scores[j], q_ref[0, :, lanes[j]], NN) for j in heads)
        dq = [dot(keys, d_scores[j], TN) for j in heads]
        for j in heads:
            if first:
                dq_acc[j] = dq[j]
            else:
                dq_acc[j] += dq[j]
        dk_acc[slot // 2, rows, :] += dk
        dv_acc[slot // 2, rows, :] += dv

    part(table[0, 2 + last], True, True)

    def step(b, carry):
        part(table[0, 2 + b], False, False)
        return carry

    lax.fori_loop(0, last, step, 0)
    for j in heads:
        grad = dq_acc[j].T * SCALE
        grad = grad * cos_ref[...] - pltpu.roll(grad, HEAD // 2, 1) * sin_ref[...]
        dq_ref[0, :, pl.ds(j * HEAD, HEAD)] = grad.astype(dq_ref.dtype)

    @pl.when(half == 1)
    def _():
        dkv_ref[:, 0, 0] = (dk_acc[...] * SCALE).astype(dkv_ref.dtype)
        dkv_ref[:, 0, 1] = dv_acc[...].astype(dkv_ref.dtype)


def attend_backward(table, queries, kv, grads, attended, lse, cosine, signed_sine, *first):
    seqs, rows, width = queries.shape
    block = rows // 2
    wide = GROUP * HEAD
    ranks = kv.shape[0]
    work = HEADS * rows * rows * ranks * seqs * 9 // 16
    rows_spec = pl.BlockSpec((1, block, wide), lambda s, g, h: (s, h, g))
    trig_spec = pl.BlockSpec((block, HEAD), lambda s, g, h: (2 * s + h, 0))
    return pl.pallas_call(
        with_tokens(backward_kernel, 9, len(first)),
        grid=(seqs, KV_HEADS, 2),
        in_specs=[
            pl.BlockSpec((1, table.shape[1]), lambda s, g, h: (s, 0), memory_space=pltpu.SMEM),
            rows_spec,
            pl.BlockSpec((ranks, 1, rows, HEAD), lambda s, g, h: (0, s, 0, g)),
            pl.BlockSpec((ranks, 1, rows, HEAD), lambda s, g, h: (0, s, 0, KV_HEADS + g)),
            rows_spec,
            rows_spec,
            pl.BlockSpec((1, 1, 1, GROUP, block), lambda s, g, h: (s, g, h, 0, 0)),
            trig_spec,
            trig_spec,
            *(pl.BlockSpec(memory_space=pl.ANY) for _ in first),
        ],
        out_specs=[
            rows_spec,
            pl.BlockSpec((ranks, 1, 2, rows, HEAD), lambda s, g, h: (0, s, 0, 0, g)),
        ],
        out_shape=[
            jax.ShapeDtypeStruct(queries.shape, jnp.bfloat16),
            jax.ShapeDtypeStruct((ranks, seqs, 2, rows, KV_HEADS * HEAD), jnp.bfloat16),
        ],
        scratch_shapes=[
            pltpu.VMEM((ranks, rows, HEAD), jnp.float32),
            pltpu.VMEM((ranks, rows, HEAD), jnp.float32),
            pltpu.VMEM((GROUP, HEAD, block), jnp.float32),
            pltpu.VMEM((GROUP, 1, block), jnp.float32),
        ],
        compiler_params=pltpu.CompilerParams(vmem_limit_bytes=40 * MIB),
        cost_estimate=cost(
            10 * HEAD * work, 12 * MIB, work
        ),
        name="attend_backward",
    )(table, queries, kv, kv, grads, attended, lse, cosine, signed_sine, *first)


def grad_kernel(count, *refs):
    kept, sent = refs[-2:]
    total = None
    for left, right in zip(refs[:count], refs[count : 2 * count]):
        term = dot(left[...], right[...], NN)
        total = term if total is None else total + term
    total = total.astype(kept.dtype)
    first = pl.program_id(0) < pl.num_programs(0) // 2

    @pl.when(first)
    def _():
        kept[...] = total

    @pl.when(jnp.logical_not(first))
    def _():
        sent[...] = total


def unit_grads(lefts, rights, *first):
    units = lefts[0].shape[0]
    rows, width = rights[0].shape
    count = len(lefts)
    block = units // 4
    half = jax.ShapeDtypeStruct((units // 2, width), jnp.bfloat16)
    return pl.pallas_call(
        with_tokens(functools.partial(grad_kernel, count), 2 * count, len(first)),
        grid=(4,),
        in_specs=[pl.BlockSpec((block, rows), lambda i: (i, 0)) for _ in lefts]
        + [pl.BlockSpec((rows, width), lambda i: (0, 0)) for _ in rights]
        + [pl.BlockSpec(memory_space=pl.ANY) for _ in first],
        out_specs=[
            pl.BlockSpec((block, width), lambda i: (jnp.minimum(i, 1), 0)),
            pl.BlockSpec((block, width), lambda i: (jnp.maximum(i - 2, 0), 0)),
        ],
        out_shape=[half, half],
        compiler_params=pltpu.CompilerParams(vmem_limit_bytes=56 * MIB),
        cost_estimate=cost(
            2 * count * units * rows * width,
            2 * count * rows * (units + width),
            0,
        ),
        name="unit_grads",
    )(*lefts, *rights, *first)


def back_kernel(count, *refs):
    out = refs[-1]
    total = None
    for left, right in zip(refs[:count], refs[count : 2 * count]):
        term = dot(left[...], right[...], TN)
        total = term if total is None else total + term
    out[...] = total.astype(out.dtype)


def back_rows(lefts, rights, *first):
    units, width = rights[0].shape
    rows = lefts[0].shape[1]
    count = len(lefts)
    block = width // 3
    return pl.pallas_call(
        with_tokens(functools.partial(back_kernel, count), 2 * count, len(first)),
        grid=(width // block,),
        in_specs=[pl.BlockSpec((units, rows), lambda i: (0, 0))] * count
        + [pl.BlockSpec((units, block), lambda i: (0, i))] * count
        + [pl.BlockSpec(memory_space=pl.ANY) for _ in first],
        out_specs=pl.BlockSpec((rows, block), lambda i: (0, i)),
        out_shape=jax.ShapeDtypeStruct((rows, width), jnp.bfloat16),
        compiler_params=pltpu.CompilerParams(vmem_limit_bytes=56 * MIB),
        cost_estimate=cost(2 * count * units * rows * width, 2 * count * units * (rows + width)),
        name="back_rows",
    )(*lefts, *rights, *first)


def hidden_kernel(rows, weight, out):
    out[...] = dot(weight[...], rows[...], NT).astype(out.dtype)


def hidden_rows(rows, weight):
    units, width = weight.shape
    count = rows.shape[0]
    block = units // 4
    return pl.pallas_call(
        hidden_kernel,
        grid=(4,),
        in_specs=[
            pl.BlockSpec((count, width), lambda i: (0, 0)),
            pl.BlockSpec((block, width), lambda i: (i, 0)),
        ],
        out_specs=pl.BlockSpec((block, count), lambda i: (i, 0)),
        out_shape=jax.ShapeDtypeStruct((units, count), jnp.bfloat16),
        compiler_params=pltpu.CompilerParams(vmem_limit_bytes=32 * MIB),
        cost_estimate=cost(2 * units * count * width, 2 * units * (count + width)),
        name="hidden_rows",
    )(rows, weight)


def project_kernel(rows_ref, gain, weight, bias, cosine, signed_sine, normed, queries, kv):
    step = pl.program_id(0)
    query_steps = pl.num_programs(0) - 2

    @pl.when(step == 0)
    def _():
        rows = rows_ref[...].astype(jnp.float32)
        scale = lax.rsqrt(jnp.mean(rows * rows, axis=-1, keepdims=True) + norm_eps)
        normed[...] = (rows * scale * gain[...]).astype(normed.dtype)

    out = dot(normed[...], weight[...], NT) + bias[...]

    def turned():
        parts = []
        for start in range(0, out.shape[1], HEAD):
            part = out[:, start : start + HEAD]
            parts.append(part * cosine[...] + pltpu.roll(part, HEAD // 2, 1) * signed_sine[...])
        return jnp.concatenate(parts, axis=1).astype(queries.dtype)

    @pl.when(step < query_steps)
    def _():
        queries[...] = turned()

    @pl.when(step == query_steps)
    def _():
        kv[...] = turned()

    @pl.when(step > query_steps)
    def _():
        kv[...] = out.astype(kv.dtype)


def project_heads(tokens, gain, weight, bias, cosine, signed_sine, *first):
    rows, width = tokens.shape
    block = KV_HEADS * HEAD
    steps = weight.shape[0] // block
    whole = pl.BlockSpec((rows, width), lambda i: (0, 0))
    table = pl.BlockSpec((rows, HEAD), lambda i: (0, 0))
    low = jnp.bfloat16
    return pl.pallas_call(
        with_tokens(project_kernel, 6, len(first)),
        grid=(steps,),
        in_specs=[
            whole,
            pl.BlockSpec((1, width), lambda i: (0, 0)),
            pl.BlockSpec((block, width), lambda i: (i, 0)),
            pl.BlockSpec((1, block), lambda i: (0, i)),
            table,
            table,
            *(pl.BlockSpec(memory_space=pl.ANY) for _ in first),
        ],
        out_specs=[
            whole,
            pl.BlockSpec((rows, block), lambda i: (0, jnp.minimum(i, steps - 3))),
            pl.BlockSpec((rows, block), lambda i: (0, jnp.maximum(i - steps + 2, 0))),
        ],
        out_shape=[
            jax.ShapeDtypeStruct((rows, width), low),
            jax.ShapeDtypeStruct((rows, (steps - 2) * block), low),
            jax.ShapeDtypeStruct((rows, 2 * block), low),
        ],
        compiler_params=pltpu.CompilerParams(vmem_limit_bytes=40 * MIB),
        cost_estimate=cost(
            2 * rows * width * weight.shape[0],
            2 * (weight.size + 4 * tokens.size),
            0,
        ),
        name="project_heads",
    )(tokens, gain, weight, bias, cosine, signed_sine, *first)


def unit_kernel(normed, d_hidden, gate, up, hidden, d_gate, d_up):
    gate_pre = dot(gate[...], normed[...], NT)
    up_pre = dot(up[...], normed[...], NT)
    d_mid = d_hidden[...].astype(jnp.float32)
    sig = 1.0 / (1.0 + jnp.exp(-gate_pre))
    silu = gate_pre * sig
    hidden[...] = (silu * up_pre).astype(hidden.dtype)
    d_up[...] = (d_mid * silu).astype(d_up.dtype)
    d_gate[...] = (d_mid * up_pre * (sig + silu * (1.0 - sig))).astype(d_gate.dtype)


def unit_rows(normed, d_hidden, gate, up):
    units, width = gate.shape
    rows = normed.shape[0]
    block = units // 4
    part = pl.BlockSpec((block, width), lambda i: (i, 0))
    out = pl.BlockSpec((block, rows), lambda i: (i, 0))
    shape = jax.ShapeDtypeStruct((units, rows), jnp.bfloat16)
    return pl.pallas_call(
        unit_kernel,
        grid=(4,),
        in_specs=[pl.BlockSpec((rows, width), lambda i: (0, 0)), out, part, part],
        out_specs=[out, out, out],
        out_shape=[shape, shape, shape],
        compiler_params=pltpu.CompilerParams(vmem_limit_bytes=60 * MIB),
        cost_estimate=cost(
            4 * units * rows * width, 4 * units * width + 8 * units * rows, 2 * units * rows
        ),
        name="unit_rows",
    )(normed, d_hidden, gate, up)


def rope_tables(positions):
    exponent = jnp.arange(0, HEAD, 2).astype(jnp.float32) / HEAD
    inverse = rope_base ** (-exponent)
    angles = positions.astype(jnp.float32)[:, None] * inverse[None, :]
    angles = jnp.concatenate([angles, angles], axis=1)
    return (jnp.cos(angles), jnp.sin(angles))


def rms_scale(values):
    return lax.rsqrt(jnp.mean(values * values, axis=-1, keepdims=True) + norm_eps)


def norm_back(d_normed, values, inv_scale, gain):
    scaled = d_normed * gain
    grad_gain = jnp.sum(d_normed * values * inv_scale, axis=0)
    inner = jnp.mean(scaled * values, axis=-1, keepdims=True)
    return (inv_scale * scaled - values * inv_scale * inv_scale * inv_scale * inner, grad_gain)


def project_rows(left, weight_rows):
    return jnp.einsum("rd,fd->rf", left, weight_rows, preferred_element_type=jnp.float32)


def flip(values, axis):
    return lax.ppermute(values, axis, [(0, 1), (1, 0)])


ALL_AXES = ("fa", "fb", "fc", "ch", "cl")
CTX_AXES = ("ch", "cl")


def over_a(values):
    if lax.axis_size("fa") == 2:
        return flip(values, "fa")
    return lax.all_gather(values, "fa", axis=0, tiled=True)


def join_a(own, other):
    return jnp.concatenate([own, other], axis=0) if lax.axis_size("fa") == 2 else other


def halves(values):
    half = values.shape[0] // 2
    return values[:half], values[half:]


def add_low(*terms):
    return functools.reduce(jnp.add, (t.astype(jnp.float32) for t in terms)).astype(jnp.bfloat16)


def add_core(kept, received):
    return [add_low(*pair) for pair in zip(halves(kept), halves(received))]


def over_a_sums(sums):
    if lax.axis_size("fa") == 2:
        return flip(sums[1], "fa")
    return lax.psum_scatter(jnp.concatenate(sums, axis=0), "fa", scatter_dimension=0, tiled=True)


def add_a(sums, received):
    return add_low(sums[0], received) if lax.axis_size("fa") == 2 else received


def core_kernel(core, left, right, kept, sent):
    total = dot(left[...], right[...], TN).astype(kept.dtype)

    @pl.when(pl.program_id(1) == 0)
    def _():
        kept[...] = total

    @pl.when(pl.program_id(1) == 1)
    def _():
        sent[...] = total


def core_terms(left, right, block, *first):
    rows, columns = left.shape
    width = right.shape[1]
    count = columns // block // 2
    me = lax.axis_index("fc")
    if block % 128:
        terms = dot(left, right, TN).astype(jnp.bfloat16).reshape(count, 2, block, width)
        pick = lambda k: lax.dynamic_index_in_dim(terms, k, 1, keepdims=False)
        return pick(me).reshape(-1, width), pick(1 - me).reshape(-1, width)
    out = pl.BlockSpec((block, width), lambda i, k, core: (i, 0))
    half = jax.ShapeDtypeStruct((count * block, width), jnp.bfloat16)
    return pl.pallas_call(
        with_tokens(core_kernel, 3, len(first)),
        grid_spec=pltpu.PrefetchScalarGridSpec(
            num_scalar_prefetch=1,
            grid=(count, 2),
            in_specs=[
                pl.BlockSpec((rows, block), lambda i, k, core: (0, 2 * i + (core[0] + k) % 2)),
                pl.BlockSpec((rows, width), lambda i, k, core: (0, 0)),
                *(pl.BlockSpec(memory_space=pl.ANY) for _ in first),
            ],
            out_specs=[out, out],
        ),
        out_shape=[half, half],
        compiler_params=pltpu.CompilerParams(vmem_limit_bytes=32 * MIB),
        cost_estimate=cost(2 * rows * columns * width, 2 * (rows + columns) * width),
        name="core_terms",
    )(me[None].astype(jnp.int32), left, right, *first)


def scatter_far(far):
    half = far.shape[0] // 2
    return flip(far[:half], "fb"), flip(far[half:], "cl")


def scatter_near(over_x, over_z, from_x, from_z):
    half = over_x.shape[0] // 2
    low, wide = jnp.bfloat16, jnp.float32
    over_x, over_z, from_x, from_z = (v.astype(wide) for v in (over_x, over_z, from_x, from_z))
    send_z = jnp.concatenate([over_z[:half] + from_x, over_z[half:]], axis=0)
    send_x = jnp.concatenate([over_x[:half], over_x[half:] + from_z], axis=0)
    return send_x.astype(low), send_z.astype(low)


def pack_vectors(vectors, blocks):
    flat = jnp.concatenate([v.reshape(blocks, -1) for v in vectors], axis=1)
    lanes = -(-flat.shape[1] // 1024) * 128
    flat = jnp.pad(flat, ((0, 0), (0, 8 * lanes - flat.shape[1])))
    return flat.reshape(blocks, 8, lanes)


def unpack_vectors(packed, sizes):
    flat = packed.reshape(packed.shape[0], -1)
    out = []
    start = 0
    for size in sizes:
        out.append(flat[:, start : start + size].reshape(-1))
        start += size
    return out


def xor_send(values, bits):
    count = lax.axis_size(CTX_AXES)
    return lax.ppermute(values, CTX_AXES, [(i, i ^ bits) for i in range(count)])


def stack_in_order(own, other, axis, dim):
    later = lax.axis_index(axis) == 1
    return jnp.stack([jnp.where(later, other, own), jnp.where(later, own, other)], axis=dim)


def stack_axis(values, axis, dim):
    if lax.axis_size(axis) == 2:
        return stack_in_order(values, flip(values, axis), axis, dim)
    return lax.all_gather(values, axis, axis=dim, tiled=False)


def order_ctx(*rel):
    high, low = lax.axis_index("ch") == 1, lax.axis_index("cl") == 1
    shape = rel[0].shape
    rel = [jnp.where(low, rel[k ^ 1], rel[k]) for k in range(4)]
    rel = [jnp.where(high, rel[k ^ 2], rel[k]) for k in range(4)]
    return jnp.stack(rel).reshape(2, 2, *shape)


def stack_plane_first(over_z):
    if lax.axis_size("fa") != 2:
        return stack_axis(over_z, "fb", 0), None
    return flip(over_z, "fa"), flip(over_z, "fb")


def stack_plane(over_z, by_a, by_b, far_top, far_bottom):
    far = jnp.concatenate([far_top, far_bottom], axis=2)
    near = stack_in_order(over_z, by_b, "fb", 0)
    beyond = stack_in_order(by_a, far, "fb", 0)
    return stack_in_order(near, beyond, "fa", 0)


def exchange(values, axes):
    return lax.all_to_all(values, axes, split_axis=0, concat_axis=0, tiled=True)


def nothing_kernel(*refs):
    pass


def gate(values, *first):
    anywhere = pl.BlockSpec(memory_space=pl.ANY)
    return pl.pallas_call(
        nothing_kernel,
        in_specs=[anywhere] * (1 + len(first)),
        out_specs=anywhere,
        out_shape=jax.ShapeDtypeStruct(values.shape, values.dtype),
        input_output_aliases={0: 0},
        cost_estimate=pl.CostEstimate(flops=0, bytes_accessed=0, transcendentals=0),
        name="gate",
    )(values, *first)


def copy_kernel(source, target):
    target[...] = source[...]


def gate_copy(values, *first):
    rows, width = values.shape
    block = rows // 2 if rows % 32 == 0 else rows
    spec = pl.BlockSpec((block, width), lambda i: (i, 0))
    return pl.pallas_call(
        with_tokens(copy_kernel, 1, len(first)),
        grid=(rows // block,),
        in_specs=[spec, *(pl.BlockSpec(memory_space=pl.ANY) for _ in first)],
        out_specs=spec,
        out_shape=jax.ShapeDtypeStruct(values.shape, values.dtype),
        cost_estimate=pl.CostEstimate(flops=0, bytes_accessed=0, transcendentals=0),
        name="gate_copy",
    )(values, *first)


def wait_kernel(source, target):
    target[...] = jnp.zeros_like(target)


def wait(first):
    return pl.pallas_call(
        wait_kernel,
        in_specs=[pl.BlockSpec(memory_space=pl.ANY)],
        out_shape=jax.ShapeDtypeStruct((8, 128), jnp.float32),
        cost_estimate=cost(10**10, 10**7),
        name="wait",
    )(first)


def on_device(
    tokens, stretch_pairs, cotangent, w_qkv, b_qkv, w_out, norm_attn, norm_mlp, w_gate, w_up, w_down
):
    ctx_count = lax.axis_size(CTX_AXES)
    device_count = lax.axis_size(ALL_AXES)
    device_grid = tuple(lax.axis_size(axis) for axis in ALL_AXES)
    ctx_rank = lax.axis_index(CTX_AXES)
    seq_count = stretch_pairs.shape[0]
    row_count, width = tokens.shape
    local_len = row_count // seq_count
    half_len = local_len // 2
    seq_len = local_len * ctx_count
    query_width = HEADS * HEAD
    kv_width = KV_HEADS * HEAD
    low, wide = jnp.bfloat16, jnp.float32

    half_rows = row_count // 2

    own_pair = lax.dynamic_slice_in_dim(stretch_pairs, ctx_rank, 1, axis=1)
    blocks = jnp.arange(2 * ctx_count)
    block_pair = jnp.minimum(blocks, 2 * ctx_count - 1 - blocks)
    holder = jnp.argmax(stretch_pairs[:, None, :] == block_pair[None, :, None], axis=2)
    slots = 2 * holder + (blocks >= ctx_count)[None, :]
    table = jnp.concatenate(
        [own_pair, 2 * ctx_count - 1 - own_pair, slots.astype(jnp.int32)], axis=1
    )
    offsets = jnp.arange(local_len)
    positions = jnp.where(
        offsets < half_len,
        own_pair * half_len + offsets,
        (2 * ctx_count - 1 - own_pair) * half_len + offsets - half_len,
    )
    cosine, sine_table = rope_tables(positions.reshape(row_count))
    signed_sine = jnp.where(jnp.arange(HEAD) < HEAD // 2, -sine_table, sine_table)

    vectors = pack_vectors([b_qkv, norm_attn, norm_mlp], 1)
    vectors_all = exchange(
        jnp.broadcast_to(vectors, (device_count, *vectors.shape[1:])), ALL_AXES
    )
    qkv_parts = [xor_send(w_qkv, k) for k in (1, 2, 3)]
    down_a = over_a(w_down)
    qkv_parts[0] = gate(qkv_parts[0], wait(w_qkv))
    qkv_z = order_ctx(w_qkv, *qkv_parts)
    by_a, by_b = stack_plane_first(qkv_z)
    own_down = gate_copy(w_down, qkv_z)
    down_z = flip(own_down, "ch")
    vectors_all = gate(vectors_all, qkv_z)
    cot_z = flip(gate_copy(cotangent, qkv_z), "cl")
    by_a = gate(by_a, wait(qkv_z), down_a)
    if by_b is None:
        qkv_plane = stack_axis(by_a, "fa", 0)
    else:
        far_top = flip(by_a[:, :, : by_a.shape[2] // 2], "fb")
        far_bottom = flip(by_b[:, :, by_b.shape[2] // 2 :], "fa")
        far_top = gate(far_top, wait(by_a))
        qkv_plane = stack_plane(qkv_z, by_a, by_b, far_top, far_bottom)
    out_all = lax.all_gather(gate_copy(w_out, qkv_plane), ALL_AXES, axis=0, tiled=True)
    cot_x = flip(gate_copy(cotangent, qkv_plane), "fb")
    own_gate = gate_copy(w_gate, qkv_plane)
    gate_a = over_a(own_gate)
    qkv_other = gate(flip(qkv_plane, "fc"), wait(qkv_plane))
    qkv_all = stack_in_order(qkv_plane, qkv_other, "fc", 2).reshape(-1, width)
    bias_all, gain_one, gain_two = unpack_vectors(
        vectors_all, (b_qkv.shape[0], norm_attn.shape[0], norm_mlp.shape[0])
    )
    gain_one, gain_two = gain_one.astype(wide)[None], gain_two.astype(wide)[None]

    normed_one, queries, kv_low = project_heads(
        tokens, gain_one, qkv_all, bias_all.astype(wide)[None], cosine, signed_sine
    )
    kv_low = kv_low.reshape(1, seq_count, local_len, 2 * kv_width)
    kv_sent = jnp.broadcast_to(kv_low, (ctx_count, *kv_low.shape[1:]))
    kv_all = exchange(kv_sent, CTX_AXES)
    gate_copied, up_copied = gate_copy(w_gate, kv_sent), gate_copy(w_up, kv_sent)
    cot_z, down_z = gate(cot_z, kv_sent, gate_copied, up_copied), gate(down_z, kv_sent)
    cot_far = flip(cot_z, "fb")
    down_az = over_a(down_z)
    own_up = gate_copy(w_up, kv_sent)
    up_a = over_a(own_up)
    cot_parts = [cotangent, cot_x, cot_z, cot_far]

    gate_z = flip(gate(gate_copied, kv_all), "ch")
    queries = queries.reshape(seq_count, local_len, query_width)
    attended, log_totals = attend_forward(
        table, queries, kv_all, wait(kv_low), cot_x, cot_far, down_az, gate_a, up_a
    )
    attended_rows = attended.reshape(row_count, query_width)

    def middle_rows(rows, weight, inputs, gain):
        middle = inputs.astype(wide) + jnp.dot(rows, weight, preferred_element_type=wide)
        scale = rms_scale(middle)
        return (middle * scale * gain).astype(low), middle, scale

    normed_two, middle, inv_two = middle_rows(attended_rows, out_all, tokens, gain_two)

    def join_units(own, by_z, by_a, by_az):
        if lax.axis_size("fa") == 2:
            return jnp.concatenate([own, by_z, by_a, by_az], axis=0)
        blocks = [block.reshape(-1, *own.shape) for block in (by_a, by_az)]
        return jnp.concatenate(blocks, axis=1).reshape(-1, width)

    def join_core(own, other):
        return jnp.concatenate([own, other], axis=0)

    normed_x, normed_z = flip(normed_two, "fb"), flip(normed_two, "cl")
    up_z = flip(gate(up_copied, attended), "ch")
    down_own = join_units(own_down, down_z, down_a, gate(down_az, normed_two))
    down_part = join_core(down_own, gate(flip(down_own, "fc"), wait(down_own)))
    d_hidden = [hidden_rows(cot, down_part) for cot in cot_parts]
    gate_z = gate(gate_z, d_hidden[0])
    gate_az = over_a(gate_z)
    normed_x, normed_z = gate(normed_x, *d_hidden), gate(normed_z, *d_hidden)
    far_top, far_bottom = flip(normed_z[:half_rows], "fb"), flip(normed_x[half_rows:], "cl")
    up_z = gate(up_z, *d_hidden)
    up_az = over_a(up_z)
    up_own = join_units(own_up, up_z, up_a, gate(up_az, *d_hidden))
    up_part = join_core(up_own, gate(flip(up_own, "fc"), wait(up_own)))
    gate_own = join_units(own_gate, gate_z, gate_a, gate(gate_az, up_own))
    gate_part = join_core(gate_own, gate(flip(gate_own, "fc"), wait(gate_own)))
    normed_far = join_core(gate(far_top, gate_own), far_bottom)
    normed_parts = [normed_two, normed_x, normed_z, normed_far]
    hidden, d_gate, d_up = zip(
        *(unit_rows(n, d, gate_part, up_part) for n, d in zip(normed_parts, d_hidden))
    )

    def back_units(k, *first):
        return back_rows((d_gate[k], d_up[k]), (gate_part, up_part), *first)

    def branch_rows(k, *first):
        return back_rows((hidden[k],), (down_part,), *first)

    back_far = back_units(3)
    back_from = scatter_far(back_far)
    back_x = back_units(1, back_far)
    back_z = back_units(2, back_x)
    back_sent = scatter_near(back_x, back_z, gate(back_from[0], back_z), back_from[1])
    back_x, back_z = flip(back_sent[0], "fb"), flip(back_sent[1], "cl")
    down_kept, down_sent = unit_grads(hidden, cot_parts, *back_sent)
    down_sent = flip(down_sent, "fc")
    back_own = back_units(0, down_kept)
    down_sums = add_core(down_kept, gate(down_sent, back_own))
    down_from_a = over_a_sums(down_sums)

    def back_norm(own, by_x, by_z, middle, scale, gain, cotangent):
        d_normed = own.astype(wide) + by_x.astype(wide) + by_z.astype(wide)
        d_rows, grad_gain = norm_back(d_normed, middle, scale, gain)
        d_middle = cotangent.astype(wide) + d_rows
        return d_middle.astype(low), d_middle, grad_gain

    d_branch, d_middle, grad_gain_two = back_norm(back_own, back_x, back_z, middle, inv_two, gain_two, cotangent
    )
    d_attended = project_rows(d_branch, out_all).astype(low)
    d_queries, d_kv_parts = attend_backward(
        table,
        queries,
        kv_all,
        d_attended.reshape(seq_count, local_len, query_width),
        attended,
        log_totals,
        cosine,
        signed_sine,
        *down_sums,
    )
    d_queries = d_queries.reshape(row_count, query_width)
    d_kv_parts = exchange(d_kv_parts, CTX_AXES)

    def add_wide(own, other):
        return own.astype(wide) + other.astype(wide)

    def split_terms(left, right, *first):
        return core_terms(left, right, ctx_count * w_qkv.shape[0], *first)

    def turn_back(parts):
        d_kv = jnp.sum(parts, axis=0, dtype=wide)
        d_keys, d_values = (d_kv[:, k].reshape(row_count, kv_width) for k in (0, 1))
        turned = []
        for start in range(0, kv_width, HEAD):
            part = d_keys[:, start : start + HEAD]
            turned.append(part * cosine - jnp.roll(part, HEAD // 2, 1) * signed_sine)
        return jnp.concatenate([*turned, d_values], axis=1).astype(low)

    gate_kept, gate_sent = unit_grads(d_gate, normed_parts, d_queries)
    gate_sent = flip(gate_sent, "fc")
    grad_out_local = back_rows((attended_rows,), (d_branch,), gate_kept)
    grad_out = lax.psum_scatter(grad_out_local, ALL_AXES, scatter_dimension=0, tiled=True)
    down_sums = add_a(down_sums, gate(down_from_a, grad_out_local))
    down_z_sums = flip(halves(down_sums)[1], "ch")
    query_kept, query_sent = split_terms(d_queries, normed_one, down_sums)
    query_sent = flip(query_sent, "fc")
    gate_sums = add_core(gate_kept, gate(gate_sent, query_kept))
    gate_from_a = over_a_sums(gate_sums)
    up_kept, up_sent = unit_grads(d_up, normed_parts, *gate_sums)
    up_sent = flip(up_sent, "fc")
    branch_far = branch_rows(3, up_kept)
    branch_from = flip(branch_far, "fb")
    branch_z = branch_rows(2, branch_far)
    d_kv = turn_back(gate(d_kv_parts, branch_z))
    query_sums = add_low(query_kept, gate(query_sent, d_kv))
    gate_sums = add_a(gate_sums, gate(gate_from_a, query_sums))
    gate_z_sums = flip(halves(gate_sums)[1], "ch")
    up_sums = add_core(up_kept, gate(up_sent, gate_sums))
    up_from_a = over_a_sums(up_sums)
    kv_kept, kv_sent = split_terms(d_kv, normed_one, *up_sums)
    kv_sent = flip(kv_sent, "fc")
    query_bias_local = jnp.sum(d_queries, axis=0, dtype=wide)
    kv_bias_local = jnp.sum(d_kv, axis=0, dtype=wide)

    def back_projection(d_queries, d_kv, weight):
        return dot(d_queries, weight[:query_width], NN) + dot(d_kv, weight[query_width:], NN)

    def back_tokens(d_normed, tokens, gain, d_middle):
        inputs = tokens.astype(wide)
        d_rows, grad_gain = norm_back(d_normed, inputs, rms_scale(inputs), gain)
        return d_middle + d_rows, grad_gain

    def join_qkv(query_sums, kept, sent):
        sums = jnp.concatenate([query_sums, add_wide(kept, sent).astype(low)], axis=0)
        return sums.reshape(-1, ctx_count, *w_qkv.shape)

    def add_all(values):
        return jnp.sum(values, axis=0, dtype=wide)

    qkv_terms = join_qkv(query_sums, kv_kept, gate(kv_sent, wait(kv_kept)))
    qkv_sums = exchange(qkv_terms, ("fa", "fb"))
    d_normed_one = back_projection(d_queries, gate(d_kv, qkv_terms), qkv_all)
    grad_tokens, grad_gain_one = back_tokens(d_normed_one, tokens, gain_one, d_middle)
    vector_grads = [query_bias_local, kv_bias_local, grad_gain_one, grad_gain_two]
    branch_x = branch_rows(1, grad_tokens)
    branch_own = branch_rows(0, branch_x)
    branch_x = flip(branch_x, "fb")
    branch_z = add_low(branch_z, gate(branch_from, branch_own))
    grad_down = add_wide(halves(down_sums)[0], gate(down_z_sums, branch_z))
    branch_z = flip(branch_z, "cl")
    up_sums = add_a(up_sums, gate(up_from_a, grad_down))
    up_z_sums = flip(halves(up_sums)[1], "ch")
    grad_gate = add_wide(halves(gate_sums)[0], gate(gate_z_sums, up_sums))
    qkv_sums = add_all(gate(qkv_sums, grad_gate)).astype(low)
    branch_sum = add_wide(branch_own, gate(branch_x, qkv_sums))
    qkv_sums = gate(qkv_sums, branch_sum)

    def pick(rank):
        return lax.dynamic_index_in_dim(qkv_sums, rank, 0, keepdims=False)

    qkv_own = pick(ctx_rank)
    qkv_from = [xor_send(pick(ctx_rank ^ k), k) for k in (1, 2, 3)]
    packed = gate(pack_vectors(vector_grads, device_count), pick(ctx_rank ^ 3))
    vector_shares = exchange(packed, ALL_AXES)
    branch_z = gate(branch_z, pick(ctx_rank ^ 2))
    layer_out = (middle + add_wide(branch_z, branch_sum)).astype(low)
    qkv_from[0] = gate(qkv_from[0], wait(qkv_own), layer_out)
    grad_out = gate(grad_out, qkv_own).astype(wide)
    grad_qkv = functools.reduce(jnp.add, (part.astype(wide) for part in (qkv_own, *qkv_from)))
    grad_up = add_wide(halves(up_sums)[0], gate(up_z_sums, grad_qkv))
    grad_query_bias, grad_kv_bias, grad_norm_attn, grad_norm_mlp = unpack_vectors(
        jnp.sum(vector_shares, axis=0)[None], [v.shape[0] // device_count for v in vector_grads]
    )
    return (
        layer_out,
        grad_tokens,
        grad_qkv,
        grad_query_bias,
        grad_kv_bias,
        grad_out,
        grad_norm_attn,
        grad_norm_mlp,
        grad_gate,
        grad_up,
        grad_down,
    )


def solution(mesh):
    fsdp_count, ctx_count = mesh.shape["fsdp"], mesh.shape["ctx"]
    parts = (fsdp_count // 4, 2, 2, ctx_count // 2, 2)
    split_mesh = Mesh(mesh.devices.reshape(parts), ALL_AXES)
    rows, whole = P(ALL_AXES, None), P(ALL_AXES)
    return jax.shard_map(
        on_device,
        mesh=split_mesh,
        in_specs=(
            rows,
            P(("fa", "fb", "fc"), None),
            rows,
            rows,
            whole,
            rows,
            whole,
            whole,
            rows,
            rows,
            rows,
        ),
        out_specs=(rows, rows, rows, whole, whole, rows, whole, whole, rows, rows, rows),
        check_vma=False,
    )
```
